32 devices in a mesh: dp: 16 (over z, y, x), tensor: 2 (over core).
Axes of the slice: x: 2, y: 2, z: 4, core: 2. Of those that a mesh axis runs over, the one named last changes fastest.
Arguments:
- inputs: bfloat16 [16384, 768], P('dp'), may hold values from -6 to 6
- seq_lengths: int32 [16, 8], P('dp'), may hold values from 0 to 1024, as said below
- qkv_weight: bfloat16 [3, 768, 768], P(None, None, 'tensor'), may hold values from -0.21875 to 0.21875
- out_weight: bfloat16 [768, 768], P('tensor'), may hold values from -1.75 to 1.75
- up_weight: bfloat16 [768, 3072], P(None, 'tensor'), may hold values from -0.21875 to 0.21875
- down_weight: bfloat16 [3072, 768], P('tensor'), may hold values from -0.109375 to 0.109375
- select_weight: bfloat16 [2, 768, 64], replicated, may hold values from -0.079589844 to 0.079589844
- norm_gains: float32 [2, 768], replicated, may hold values from 0.5 to 1.5
- grad_output: bfloat16 [16384, 768], P('dp'), may hold values from -6 to 6
Outputs:
- output: bfloat16 [16384, 768], P('dp')
- grad_inputs: float32 [16384, 768], P('dp')
- grad_qkv: float32 [3, 768, 768], P(None, None, 'tensor')
- grad_out: float32 [768, 768], P('tensor')
- grad_up: float32 [768, 3072], P(None, 'tensor')
- grad_down: float32 [3072, 768], P('tensor')
- grad_select: float32 [2, 768, 64], replicated
- grad_gains: float32 [2, 768], replicated
The draws below stay inside these ranges and needn't reach their ends.
Inputs may be any that keep to these rules, and one draw needn't show every extreme that they name: `seq_lengths`: each row lists up to 8 sequences packed in order into one dp index's 1024 slots: every length is a multiple of 128, zeros stand only after the last sequence, the first is at least 128, a row sums to 512 or more and at most 1024; some row holds a single sequence of 1024.
All inputs are finite; a program needn't handle non-finite values.
Results may differ from the reference program's by a relative error of at most 0.015.
The reference program's roundings to bfloat16 on the way count: a program that leaves them out, or rounds other values in their place, can miss the bound.
Values may be sent and summed in bfloat16 or wider, within the bound.
No kernel may reach another device: no remote copies, remote signals or barrier semaphores. Data moves between devices by JAX's collectives and lax.ppermute only.
A program may use at most 192 MiB of HBM per device.

```python
import jax
import jax.numpy as jnp
from jax import lax

D = 768
HD = 64
FF = 3072
TOK_DEV = 1024
SEQS = 8
BUCKET = 128
TOKENS = 16384
N_DP = 16
N_TENSOR = 2


def draw_seq_lengths(key, part):
    key_steps, key_fill, key_row = jax.random.split(key, 3)
    block_total = TOK_DEV // BUCKET
    powers = jax.random.randint(key_steps, (N_DP, SEQS), 0, 4)
    steps_taken = jnp.left_shift(jnp.ones((N_DP, SEQS), jnp.int32), powers)
    fill_blocks = jax.random.randint(key_fill, (N_DP, 1), block_total // 2, block_total + 1)
    seq_ends = jnp.minimum(jnp.cumsum(steps_taken, axis=1), fill_blocks)
    seq_starts = jnp.concatenate([jnp.zeros((N_DP, 1), jnp.int32), seq_ends[:, :-1]], axis=1)
    lengths_all = (seq_ends - seq_starts) * BUCKET
    full_row = jax.random.randint(key_row, (), 0, N_DP)
    single_row = jnp.zeros((SEQS,), jnp.int32).at[0].set(TOK_DEV)
    row_ids = jnp.arange(N_DP, dtype=jnp.int32)[:, None]
    return jnp.where(row_ids == full_row, single_row[None, :], lengths_all).astype(jnp.int32)


def steps_of(rng, extent, cuts, smallest, high):
    gain, own = 1.0, jax.random.fold_in(rng, 6)
    for position, blocks in cuts:
        heights = jnp.exp(jax.random.uniform(jax.random.fold_in(own, position), (blocks,), jnp.float32, smallest / len(cuts), high / len(cuts)))
        gain = gain * jnp.repeat(heights, extent[position] // blocks).reshape([-1 if axis == position else 1 for axis in range(len(extent))])
    return gain


def normal_values(own_key, extent, width, bound, shards=(), kind=jnp.bfloat16):
    entries = width * jax.random.normal(own_key, extent, jnp.float32)
    if shards:
        entries = entries * steps_of(own_key, extent, shards, -0.22, 0.18)
    return jnp.clip(entries, -bound, bound).astype(kind)


def setup_inputs(seed: int = 0) -> dict:
    key_of = jax.random.split(jax.random.key(seed), 10)
    return {
        "inputs": normal_values(key_of[0], (TOKENS, D), 1.0, 6.0, ((0, 16),)),
        "seq_lengths": draw_seq_lengths(jax.random.fold_in(key_of[9], 71), 0),
        "qkv_weight": normal_values(key_of[2], (3, D, D), D ** -0.5, 0.21875, ((2, 2),)),
        "out_weight": normal_values(key_of[3], (D, D), (D // 64) ** -0.5, 1.75, ((0, 2),)),
        "up_weight": normal_values(key_of[4], (D, FF), D ** -0.5, 0.21875, ((1, 2),)),
        "down_weight": normal_values(key_of[5], (FF, D), FF ** -0.5, 0.109375, ((0, 2),)),
        "select_weight": normal_values(key_of[6], (2, D, HD), 0.011, 0.079589844),
        "norm_gains": jnp.clip(1.0 + 0.1 * jax.random.normal(key_of[7], (2, D), jnp.float32), 0.5, 1.5),
        "grad_output": normal_values(key_of[8], (TOKENS, D), 1.0, 6.0, ((0, 16),)),
    }


@jax.custom_vjp
def low(v):
    return lax.optimization_barrier(v.astype(jnp.bfloat16)).astype(jnp.float32)

@jax.custom_vjp
def low_back(v):
    return v

def low_keep(v):
    return (low(v), None)

def low_pass(kept, grad):
    return (grad,)

def back_keep(v):
    return (v, None)

def back_low(kept, grad):
    return (low(grad),)
low.defvjp(low_keep, low_pass)
low_back.defvjp(back_keep, back_low)
highest = lax.Precision.HIGHEST

def rms_norm(values, gain_vec):
    return values * lax.rsqrt(lax.optimization_barrier(jnp.mean(values * values, axis=-1, keepdims=True)) + 1e-06) * gain_vec

def gelu_curve(values):
    return 0.5 * values * (1.0 + jnp.tanh(0.7978845608028654 * (values + 0.044715 * values * values * values)))

def seq_masks(lengths_row, row_count):
    positions = jnp.arange(row_count, dtype=jnp.int32)
    seq_ends = jnp.cumsum(lengths_row)
    seq_starts = seq_ends - lengths_row
    segment = lax.optimization_barrier(jnp.sum((positions[:, None] >= seq_ends[None, :]).astype(jnp.int32), axis=1))
    is_valid = positions < seq_ends[-1]
    is_first = jnp.any((positions[:, None] == seq_starts[None, :]) & (lengths_row[None, :] > 0), axis=1)
    same_seq = (segment[:, None] == segment[None, :]) & is_valid[:, None]
    earlier = positions[None, :] < positions[:, None]
    attend = same_seq & earlier | (positions[:, None] == positions[None, :])
    chosen = same_seq & earlier & jnp.logical_not(is_first)[None, :]
    return (attend, chosen)

def group_attention(h_low, w_group, w_select, attend, chosen):
    row_count = h_low.shape[0]
    score_scale = HD ** (-0.5)
    queries = low(low_back(jnp.dot(h_low, w_group[0], precision=highest)))
    key_rows = low(low_back(jnp.dot(h_low, w_group[1], precision=highest)))
    value_rows = low(low_back(jnp.dot(h_low, w_group[2], precision=highest)))
    head_count = queries.shape[1] // HD
    sel_query = low(low_back(jnp.dot(h_low, w_select[0], precision=highest)))
    sel_key = low(low_back(jnp.dot(h_low, w_select[1], precision=highest)))
    select_score = low_back(jnp.dot(sel_query, sel_key.T, precision=highest) * score_scale)
    positive = jax.nn.relu(select_score)
    picked = jnp.where(chosen, positive * positive, 0.0)
    running = jnp.cumsum(picked, axis=0)
    penalty = jnp.concatenate([jnp.zeros((1, row_count), picked.dtype), running[:-1]], axis=0)
    q_heads = queries.reshape(row_count, head_count, HD)
    k_heads = key_rows.reshape(row_count, head_count, HD)
    v_heads = value_rows.reshape(row_count, head_count, HD)
    scores = low_back(jnp.einsum('qhd,khd->hqk', q_heads, k_heads, precision=highest) * score_scale) - penalty[None]
    scores = jnp.where(attend[None], scores, -1e+30)
    attn_probs = jax.nn.softmax(scores, axis=-1)
    mixed_heads = jnp.einsum('hqk,khd->qhd', low(attn_probs), v_heads, precision=highest)
    return low(low_back(mixed_heads)).reshape(row_count, head_count * HD)

def reference(inputs, seq_lengths, qkv_weight, out_weight, up_weight, down_weight, select_weight, norm_gains, grad_output):
    groups = N_TENSOR
    half_width = D // groups
    half_hidden = FF // groups

    def forward(xin, w_qkv_full, w_out_full, w_up_full, w_down_full, w_select, gains_full):
        w_groups = [w_qkv_full[:, :, group * half_width:(group + 1) * half_width] for group in range(groups)]

        def buffer_layer(pieces):
            x_rows, lengths_row = pieces
            attend, chosen = seq_masks(lengths_row, TOK_DEV)
            normed_one = rms_norm(x_rows, gains_full[0])
            attn_sum = jnp.zeros_like(x_rows)
            for group in range(groups):
                h_one = low(low_back(normed_one))
                mixed = group_attention(h_one, w_groups[group], w_select, attend, chosen)
                part = jnp.dot(mixed, w_out_full[group * half_width:(group + 1) * half_width], precision=highest)
                attn_sum = attn_sum + low(low_back(part))
            middle = x_rows + attn_sum
            normed_two = rms_norm(middle, gains_full[1])
            branch = jnp.zeros_like(x_rows)
            for group in range(groups):
                h_two = low(low_back(normed_two))
                up_values = jnp.dot(h_two, w_up_full[:, group * half_hidden:(group + 1) * half_hidden], precision=highest)
                active = low(gelu_curve(low_back(up_values)))
                part = jnp.dot(active, w_down_full[group * half_hidden:(group + 1) * half_hidden], precision=highest)
                branch = branch + low(low_back(part))
            return middle + branch
        rows_all = lax.map(jax.checkpoint(buffer_layer), (xin.reshape(N_DP, TOK_DEV, D), seq_lengths))
        return rows_all.reshape(N_DP * TOK_DEV, D)
    primals = (inputs.astype(jnp.float32), qkv_weight.astype(jnp.float32), out_weight.astype(jnp.float32), up_weight.astype(jnp.float32), down_weight.astype(jnp.float32), select_weight.astype(jnp.float32), norm_gains.astype(jnp.float32))
    result, pull_back = jax.vjp(forward, *primals)
    grads = pull_back(grad_output.astype(jnp.float32))
    return (result.astype(jnp.bfloat16), grads[0], grads[1], grads[2], grads[3], grads[4], grads[5], grads[6])
```

```python
import functools

import jax
import jax.numpy as jnp
from jax import lax
from jax.experimental import pallas as pl
from jax.experimental.pallas import tpu as pltpu
from jax.sharding import PartitionSpec as P

BF = jnp.bfloat16
F32 = jnp.float32
EPS = 1e-6
BLK = 256
NOT_ATTENDED = 1e30
CURVE = 0.7978845608028654
CUBE = 0.044715
MIB = 1024 * 1024


def mm(a, b):
    return jnp.dot(a, b, preferred_element_type=F32)


def mm_nt(a, b):
    return lax.dot_general(a, b, (((1,), (1,)), ((), ())), preferred_element_type=F32)


def mm_tn(a, b):
    return lax.dot_general(a, b, (((0,), (0,)), ((), ())), preferred_element_type=F32)


def params(limit_mib=56):
    return pltpu.CompilerParams(
        dimension_semantics=("arbitrary",), vmem_limit_bytes=limit_mib * MIB
    )


def cost(flops, nbytes, trans=0):
    return pl.CostEstimate(flops=int(flops), bytes_accessed=int(nbytes), transcendentals=int(trans))


def shape(dims, dtype):
    return jax.ShapeDtypeStruct(tuple(dims), dtype)


def whole(*dims):
    return pl.BlockSpec(tuple(dims), lambda *_: (0,) * len(dims))


def rows(width, count=BLK):
    return pl.BlockSpec((count, width), lambda i, *_: (i, 0))


def smem():
    return pl.BlockSpec(memory_space=pltpu.SMEM)


def sequence_ids(lens, pos):
    seg = jnp.zeros(pos.shape, jnp.int32)
    first = jnp.zeros(pos.shape, jnp.bool_)
    end = jnp.int32(0)
    for s in range(lens.shape[1]):
        length = lens[0, s]
        first = first | ((pos == end) & (length > 0))
        end = end + length
        seg = seg + (pos >= end).astype(jnp.int32)
    seg = jnp.where(pos < end, seg, lens.shape[1] + 1 + pos)
    return seg, first


def masks_t(lens, start, width):
    col = lax.broadcasted_iota(jnp.int32, (width, 1), 0)
    row = start + lax.broadcasted_iota(jnp.int32, (1, BLK), 1)
    seg_j, first_j = sequence_ids(lens, col)
    seg_i, _ = sequence_ids(lens, row)
    attend = (seg_j == seg_i) & (col <= row)
    chosen = (jnp.where(first_j, -1, seg_j) == seg_i) & (col < row)
    return attend, chosen


def split_dot(values, ones):
    high = values.astype(BF)
    low = (values - high.astype(F32)).astype(BF)
    return mm(high, ones) + mm(low, ones)


def norm_scale(values):
    return lax.rsqrt(jnp.mean(values * values, axis=-1, keepdims=True) + EPS)


def forward_kernel(
    n_blocks, heads, lens, x, gains, wqkv, wsel_t, wout,
    h1_o, q_o, k_o, v_o, sq_o, sk_o, pen_o, lse_o, mix_o, part_o,
    k_s, vt_s, sk_s, carry_s,
):
    step = pl.program_id(0)
    hd = wsel_t.shape[1]
    scale = hd**-0.5
    xf = x[...].astype(F32)
    h1 = (xf * norm_scale(xf) * gains[0:1, :]).astype(BF)
    h1_o[...] = h1
    q = (mm(h1, wqkv[0]).astype(BF) * scale).astype(BF)
    k = mm(h1, wqkv[1]).astype(BF)
    v32 = mm(h1, wqkv[2])
    v = v32.astype(BF)
    sq = (mm_nt(h1, wsel_t[0]).astype(BF) * scale).astype(BF)
    sk = mm_nt(h1, wsel_t[1]).astype(BF)
    q_o[...] = q
    k_o[...] = k
    v_o[...] = v
    sq_o[...] = sq
    sk_o[...] = sk
    here = pl.ds(pl.multiple_of(step * BLK, BLK), BLK)
    k_s[here, :] = k
    sk_s[here, :] = sk
    vt_s[:, here] = v32.T.astype(BF)

    @pl.when(step == 0)
    def _():
        carry_s[...] = jnp.zeros_like(carry_s)

    lane = lax.broadcasted_iota(jnp.int32, (1, 2 * hd), 1)
    before = lax.broadcasted_iota(jnp.int32, (BLK, BLK), 0) < lax.broadcasted_iota(
        jnp.int32, (BLK, BLK), 1
    )
    before = jnp.where(before, 1.0, 0.0).astype(BF)

    def block(i):
        width = (i + 1) * BLK
        attend, chosen = masks_t(lens, i * BLK, width)
        sel = jnp.maximum(mm_nt(sk_s[:width, :], sq), 0.0)
        picked = jnp.where(chosen, sel * sel, 0.0)
        carry = carry_s[:width, 0:1]
        pen = split_dot(picked, before) + carry
        carry_s[:width, 0:1] = carry + jnp.sum(picked, axis=1, keepdims=True)
        pen_o[:width, :] = jnp.where(attend, pen, NOT_ATTENDED)
        mixed_t = []
        for h in range(heads):
            pair = slice((h // 2) * 2 * hd, (h // 2 + 1) * 2 * hd)
            mine = (lane // hd) == (h % 2)
            q_h = jnp.where(mine, q[:, pair], jnp.zeros((), BF))
            s = mm_nt(k_s[:width, pair], q_h) - pen_o[:width, :]
            top = jnp.max(s, axis=0, keepdims=True)
            p = jnp.exp(s - top)
            total = jnp.sum(p, axis=0, keepdims=True)
            lse_o[h : h + 1, :] = top + jnp.log(total)
            m_t = mm(vt_s[h * hd : (h + 1) * hd, :width], p.astype(BF))
            mixed_t.append(m_t / total)
        mixed = jnp.concatenate(mixed_t, axis=0).T.astype(BF)
        mix_o[...] = mixed
        part_o[...] = mm(mixed, wout[...]).astype(BF)

    for i in range(n_blocks):
        pl.when(step == i)(functools.partial(block, i))


def forward(lens, x, gains, wqkv, wsel_t, wout):
    t, d = x.shape
    wh = wqkv.shape[2]
    hd = wsel_t.shape[1]
    heads = wh // hd
    n = t // BLK
    tall = pl.BlockSpec((t, BLK), lambda i: (0, i))
    return pl.pallas_call(
        functools.partial(forward_kernel, n, heads),
        grid=(n,),
        in_specs=[
            smem(), rows(d), whole(*gains.shape), whole(*wqkv.shape), whole(*wsel_t.shape),
            whole(*wout.shape),
        ],
        out_specs=[
            rows(d), rows(wh), rows(wh), rows(wh), rows(hd), rows(hd), tall,
            pl.BlockSpec((8, BLK), lambda i: (0, i)), rows(wh), rows(d),
        ],
        out_shape=[
            shape((t, d), BF), shape((t, wh), BF), shape((t, wh), BF), shape((t, wh), BF),
            shape((t, hd), BF), shape((t, hd), BF), shape((t, t), F32), shape((8, t), F32),
            shape((t, wh), BF), shape((t, d), BF),
        ],
        scratch_shapes=[
            pltpu.VMEM((t, wh), BF), pltpu.VMEM((wh, t), BF), pltpu.VMEM((t, hd), BF),
            pltpu.VMEM((t, 128), F32),
        ],
        compiler_params=params(),
        cost_estimate=cost(2 * t * d * (4 * wh + 2 * hd) + 4 * heads * t * t * hd, 16 * MIB, heads * t * t),
        name="attention_forward",
    )(lens, x, gains, wqkv, wsel_t, wout)


def feed_kernel(x, part_a, part_b, gains, up, down, g, mid_o, h2_o, act_o, du_o, dn_o):
    mid = x[...].astype(F32) + (part_a[...].astype(F32) + part_b[...].astype(F32))
    mid_o[...] = mid
    h2 = (mid * norm_scale(mid) * gains[1:2, :]).astype(BF)
    h2_o[...] = h2
    hidden = up.shape[1]
    chunk = 512
    dn = jnp.zeros(mid.shape, F32)
    for c in range(hidden // chunk):
        cut = slice(c * chunk, (c + 1) * chunk)
        u = mm(h2, up[:, cut])
        da = mm_nt(g[...], down[cut, :])
        u2 = u * u
        curve = jnp.tanh(u * (CURVE + (CURVE * CUBE) * u2))
        half = 0.5 * (1.0 + curve)
        act_o[:, cut] = (u * half).astype(BF)
        slope = half + (0.5 * u) * (1.0 - curve * curve) * (CURVE + (3.0 * CURVE * CUBE) * u2)
        du = (da * slope).astype(BF)
        du_o[:, cut] = du
        dn = dn + mm_nt(du, up[:, cut])
    dn_o[...] = dn.astype(BF)


def feed(x, part_a, part_b, gains, up, down, g):
    t, d = x.shape
    hidden = up.shape[1]
    return pl.pallas_call(
        feed_kernel,
        grid=(t // BLK,),
        in_specs=[
            rows(d), rows(d), rows(d), whole(*gains.shape), whole(*up.shape), whole(*down.shape),
            rows(d),
        ],
        out_specs=[rows(d), rows(d), rows(hidden), rows(hidden), rows(d)],
        out_shape=[
            shape((t, d), F32), shape((t, d), BF), shape((t, hidden), BF), shape((t, hidden), BF),
            shape((t, d), BF),
        ],
        compiler_params=params(),
        cost_estimate=cost(6 * t * d * hidden, 20 * MIB, t * hidden),
        name="feed_forward",
    )(x, part_a, part_b, gains, up, down, g)


def product_kernel(half, left, right, out):
    out[...] = mm_tn(left[...], right[...]).astype(BF)


def weight_half(half, left, right, tile, name):
    t, m = left.shape
    n = right.shape[1]
    tiles = m // 2 // tile
    return pl.pallas_call(
        product_kernel,
        grid_spec=pltpu.PrefetchScalarGridSpec(
            num_scalar_prefetch=1,
            grid=(tiles,),
            in_specs=[
                pl.BlockSpec((t, tile), lambda j, half: (0, half[0] * tiles + j)),
                whole(t, n),
            ],
            out_specs=pl.BlockSpec((tile, n), lambda j, half: (j, 0)),
        ),
        out_shape=shape((m // 2, n), BF),
        compiler_params=params(),
        cost_estimate=cost(t * m * n, 2 * (t * m // 2 + t * n + m * n // 2)),
        name=name,
    )(half, left, right)


def norm_back(values, scale, gain, grad):
    unit = values * scale
    grad_unit = grad * gain
    mean = jnp.mean(grad_unit * unit, axis=-1, keepdims=True)
    return scale * (grad_unit - unit * mean), jnp.sum(grad * unit, axis=0, keepdims=True)


def middle_kernel(mid, part_a, part_b, gains, g, wout, dmid_o, gm_o, dmix_o, gain_o):
    values = mid[...]
    grad = part_a[...].astype(F32) + part_b[...].astype(F32)
    back, gain_grad = norm_back(values, norm_scale(values), gains[1:2, :], grad)
    dmid = g[...].astype(F32) + back
    dmid_o[...] = dmid
    gm = dmid.astype(BF)
    gm_o[...] = gm
    dmix_o[...] = mm_nt(gm, wout[...]).astype(BF)

    @pl.when(pl.program_id(0) == 0)
    def _():
        gain_o[...] = jnp.zeros_like(gain_o)

    gain_o[0:1, :] += gain_grad


def middle(mid, part_a, part_b, gains, g, wout):
    t, d = mid.shape
    wh = wout.shape[0]
    return pl.pallas_call(
        middle_kernel,
        grid=(t // BLK,),
        in_specs=[rows(d), rows(d), rows(d), whole(*gains.shape), rows(d), whole(*wout.shape)],
        out_specs=[rows(d), rows(d), rows(wh), whole(8, d)],
        out_shape=[shape((t, d), F32), shape((t, d), BF), shape((t, wh), BF), shape((8, d), F32)],
        compiler_params=params(),
        cost_estimate=cost(2 * t * d * wh, 14 * MIB),
        name="second_norm_backward",
    )(mid, part_a, part_b, gains, g, wout)


def backward_kernel(
    n_blocks, heads, lens, q, k, v, sq, sk, pen, lse, dmix, cat_o,
    kt_s, skt_s, dk_s, dv_s, dsk_s, dpen_s, carry_s,
):
    step = pl.program_id(0)
    wh = k.shape[1]
    hd = sk.shape[1]
    scale = hd**-0.5

    @pl.when(step == 0)
    def _():
        kt_s[...] = k[...].astype(F32).T.astype(BF)
        skt_s[...] = sk[...].astype(F32).T.astype(BF)
        dk_s[...] = jnp.zeros_like(dk_s)
        dv_s[...] = jnp.zeros_like(dv_s)
        dsk_s[...] = jnp.zeros_like(dsk_s)
        carry_s[...] = jnp.zeros_like(carry_s)

    lane = lax.broadcasted_iota(jnp.int32, (1, 2 * hd), 1)
    after = lax.broadcasted_iota(jnp.int32, (BLK, BLK), 0) > lax.broadcasted_iota(
        jnp.int32, (BLK, BLK), 1
    )
    after = jnp.where(after, 1.0, 0.0).astype(BF)

    def block(i):
        width = (i + 1) * BLK
        here = slice(i * BLK, width)
        dq_t = []
        for p in range(heads // 2):
            pair = slice(p * 2 * hd, (p + 1) * 2 * hd)
            q_pair, d_pair = q[:, pair], dmix[:, pair]
            k_pair, v_pair = k[:width, pair], v[:width, pair]
            probs, scores, q_both, d_both = [], [], [], []
            for side in range(2):
                h = 2 * p + side
                mine = (lane // hd) == side
                q_h = jnp.where(mine, q_pair, jnp.zeros((), BF))
                d_h = jnp.where(mine, d_pair, jnp.zeros((), BF))
                s = mm_nt(k_pair, q_h) - pen[:width, :]
                prob = jnp.exp(s - lse[h : h + 1, :])
                dprob = mm_nt(v_pair, d_h)
                dots = jnp.sum(prob * dprob, axis=0, keepdims=True)
                dscore = prob * (dprob - dots)
                if h == 0:
                    dpen_s[:width, :] = dscore
                else:
                    dpen_s[:width, :] += dscore
                low = dscore.astype(BF)
                dq_t.append(mm(kt_s[h * hd : (h + 1) * hd, :width], low))
                probs.append(prob.astype(BF))
                scores.append(low)
                q_both.append(q_h)
                d_both.append(d_h)
            dv_s[:width, pair] += mm(
                jnp.concatenate(probs, axis=1), jnp.concatenate(d_both, axis=0)
            )
            dk_s[:width, pair] += mm(
                jnp.concatenate(scores, axis=1), jnp.concatenate(q_both, axis=0)
            )
        dq = jnp.concatenate(dq_t, axis=0) * scale
        cat_o[here, 0:wh] = dq.T.astype(BF)
        _, chosen = masks_t(lens, i * BLK, width)
        dpen = dpen_s[:width, :]
        carry = carry_s[:width, 0:1]
        dpicked = split_dot(dpen, after) + carry
        carry_s[:width, 0:1] = carry + jnp.sum(dpen, axis=1, keepdims=True)
        sel = jnp.maximum(mm_nt(sk[:width, :], sq[...]), 0.0)
        dsel = jnp.where(chosen, -2.0 * dpicked * sel, 0.0).astype(BF)
        dsk_s[:width, :] += mm(dsel, sq[...])
        dsq = mm(skt_s[:, :width], dsel) * scale
        cat_o[here, 3 * wh : 3 * wh + hd] = dsq.T.astype(BF)

    for i in range(n_blocks):
        pl.when(step == n_blocks - 1 - i)(functools.partial(block, i))

    @pl.when(step == n_blocks - 1)
    def _():
        cat_o[:, wh : 2 * wh] = dk_s[...].astype(BF)
        cat_o[:, 2 * wh : 3 * wh] = dv_s[...].astype(BF)
        cat_o[:, 3 * wh + hd : 3 * wh + 2 * hd] = dsk_s[...].astype(BF)


def backward(lens, q, k, v, sq, sk, pen, lse, dmix):
    t, wh = q.shape
    hd = sq.shape[1]
    heads = wh // hd
    n = t // BLK
    width = 3 * wh + 2 * hd

    def back_rows(cols):
        return pl.BlockSpec((BLK, cols), lambda i: (n - 1 - i, 0))

    return pl.pallas_call(
        functools.partial(backward_kernel, n, heads),
        grid=(n,),
        in_specs=[
            smem(), back_rows(wh), whole(t, wh), whole(t, wh), back_rows(hd), whole(t, hd),
            pl.BlockSpec((t, BLK), lambda i: (0, n - 1 - i)),
            pl.BlockSpec((8, BLK), lambda i: (0, n - 1 - i)),
            back_rows(wh),
        ],
        out_specs=whole(t, width),
        out_shape=shape((t, width), BF),
        scratch_shapes=[
            pltpu.VMEM((wh, t), BF), pltpu.VMEM((hd, t), BF), pltpu.VMEM((t, wh), F32),
            pltpu.VMEM((t, wh), F32), pltpu.VMEM((t, hd), F32), pltpu.VMEM((t, BLK), F32),
            pltpu.VMEM((t, 128), F32),
        ],
        compiler_params=params(),
        cost_estimate=cost(10 * heads * t * t * hd, 12 * MIB, heads * t * t),
        name="attention_backward",
    )(lens, q, k, v, sq, sk, pen, lse, dmix)


def grads_kernel(half, h1, cat, mixed, gm, out):
    wide = cat.shape[1]
    out[:, :wide] = mm_tn(h1[...], cat[...]).astype(BF)
    out[:, wide:] = mm_tn(mixed[...], gm[...]).astype(BF)


def attention_weight_half(half, h1, cat, mixed, gm):
    t, d = h1.shape
    wide = cat.shape[1]
    wh = mixed.shape[1]
    tile = 128
    tiles = d // 2 // tile
    return pl.pallas_call(
        grads_kernel,
        grid_spec=pltpu.PrefetchScalarGridSpec(
            num_scalar_prefetch=1,
            grid=(tiles,),
            in_specs=[
                pl.BlockSpec((t, tile), lambda j, half: (0, half[0] * tiles + j)),
                whole(t, wide),
                pl.BlockSpec((t, tile), lambda j, half: (0, j)),
                pl.BlockSpec((t, d // 2), lambda j, half: (0, half[0])),
            ],
            out_specs=pl.BlockSpec((tile, wide + d // 2), lambda j, half: (j, 0)),
        ),
        out_shape=shape((d // 2, wide + d // 2), BF),
        compiler_params=params(),
        cost_estimate=cost(t * d * wide + t * wh * d, 6 * MIB),
        name="attention_weight_grads",
    )(half, h1, cat, mixed, gm)


def first_kernel(cat, wqkv, wsel, out):
    wh = wqkv.shape[2]
    total = mm(cat[:, 3 * wh :], wsel[...])
    for i in range(3):
        total = total + mm_nt(cat[:, i * wh : (i + 1) * wh], wqkv[i])
    out[...] = total.astype(BF)


def first_grad(cat, wqkv, wsel):
    t, width = cat.shape
    d = wqkv.shape[1]
    return pl.pallas_call(
        first_kernel,
        grid=(t // BLK,),
        in_specs=[rows(width), whole(*wqkv.shape), whole(*wsel.shape)],
        out_specs=rows(d),
        out_shape=shape((t, d), BF),
        compiler_params=params(),
        cost_estimate=cost(2 * t * d * width, 6 * MIB),
        name="first_norm_grad",
    )(cat, wqkv, wsel)


def inputs_kernel(x, part_a, part_b, gains, dmid, out, gain_o):
    values = x[...].astype(F32)
    grad = part_a[...].astype(F32) + part_b[...].astype(F32)
    back, gain_grad = norm_back(values, norm_scale(values), gains[0:1, :], grad)
    out[...] = dmid[...] + back

    @pl.when(pl.program_id(0) == 0)
    def _():
        gain_o[...] = jnp.zeros_like(gain_o)

    gain_o[0:1, :] += gain_grad


def inputs_grad(x, part_a, part_b, gains, dmid):
    t, d = x.shape
    return pl.pallas_call(
        inputs_kernel,
        grid=(t // BLK,),
        in_specs=[rows(d), rows(d), rows(d), whole(*gains.shape), rows(d)],
        out_specs=[rows(d), whole(8, d)],
        out_shape=[shape((t, d), F32), shape((8, d), F32)],
        compiler_params=params(),
        cost_estimate=cost(20 * t * d, 11 * MIB),
        name="first_norm_backward",
    )(x, part_a, part_b, gains, dmid)


def branch_kernel(act, down, out):
    out[...] = mm(act[...], down[...]).astype(BF)


def branch(act, down):
    t, hidden = act.shape
    d = down.shape[1]
    return pl.pallas_call(
        branch_kernel,
        grid=(t // BLK,),
        in_specs=[rows(hidden), whole(*down.shape)],
        out_specs=rows(d),
        out_shape=shape((t, d), BF),
        compiler_params=params(),
        cost_estimate=cost(2 * t * d * hidden, 8 * MIB),
        name="down_projection",
    )(act, down)


class Sum:
    def __init__(self, n_dp, n_tensor):
        self.n_dp, self.n_tensor = n_dp, n_tensor
        bits = [1 << b for b in range(n_dp.bit_length() - 1)]
        swapped = bits[1::-1] + bits[2:]
        self.orders = [bits if t % 2 == 0 else swapped for t in range(n_tensor)]
        self.stages = len(bits)
        self.dp = lax.axis_index("dp")
        self.tensor = lax.axis_index("tensor")

    def side(self, stage):
        sides = [(self.dp // order[stage]) % 2 for order in self.orders]
        return functools.reduce(
            lambda rest, t: jnp.where(self.tensor == t, sides[t], rest),
            range(1, self.n_tensor), sides[0],
        )

    def swap(self, value, stage):
        pairs = [
            (i * self.n_tensor + t, (i ^ self.orders[t][stage]) * self.n_tensor + t)
            for i in range(self.n_dp)
            for t in range(self.n_tensor)
        ]
        return lax.ppermute(value, ("dp", "tensor"), pairs)

    def scatter(self, send, keep):
        for stage in range(self.stages):
            got = self.swap(send, stage)
            if stage + 1 == self.stages:
                return (keep.astype(F32) + got.astype(F32)).astype(BF)
            half = keep.shape[0] // 2
            side = self.side(stage + 1)
            def part(which):
                cut = [lax.dynamic_slice_in_dim(v, which * half, half, 0) for v in (keep, got)]
                return (cut[0].astype(F32) + cut[1].astype(F32)).astype(BF)
            send, keep = part(1 - side), part(side)

    def gather(self, piece):
        for stage in reversed(range(self.stages)):
            got = self.swap(piece, stage)
            if stage == 0:
                return piece, got
            side = self.side(stage)
            low = jnp.where(side == 0, piece, got)
            piece = jnp.concatenate([low, jnp.where(side == 0, got, piece)], axis=0)


def swap_tensor(value, n_tensor):
    return lax.ppermute(value, "tensor", [(t, t ^ 1) for t in range(n_tensor)])


def join_kernel(side, mine, other, out):
    @pl.when(pl.program_id(0) == 0)
    def _():
        out[...] = mine[...].astype(F32)

    @pl.when(pl.program_id(0) == 1)
    def _():
        out[...] = other[...].astype(F32)


def join(side, mine, other):
    r, n = mine.shape
    tiles = 3
    tile = r // tiles
    return pl.pallas_call(
        join_kernel,
        grid_spec=pltpu.PrefetchScalarGridSpec(
            num_scalar_prefetch=1,
            grid=(2, tiles),
            in_specs=[
                pl.BlockSpec((tile, n), lambda s, j, side: (jnp.where(s == 0, j, tiles - 1), 0)),
                pl.BlockSpec((tile, n), lambda s, j, side: (jnp.where(s == 0, 0, j), 0)),
            ],
            out_specs=pl.BlockSpec(
                (tile, n), lambda s, j, side: (jnp.where(s == 0, side[0], 1 - side[0]) * tiles + j, 0)
            ),
        ),
        out_shape=shape((2 * r, n), F32),
        compiler_params=pltpu.CompilerParams(
            dimension_semantics=("arbitrary", "arbitrary"), vmem_limit_bytes=32 * MIB
        ),
        cost_estimate=cost(0, 12 * r * n),
        name="join_halves",
    )(side, mine, other)


def join_attention_kernel(wh, side, mine, other, qkv_o, out_o, sel_o):
    def put(piece):
        for i in range(3):
            qkv_o[i] = piece[:, i * wh : (i + 1) * wh].astype(F32)
        wide = piece.shape[1] - out_o.shape[1]
        sel_o[...] = piece[:, 3 * wh : wide].astype(F32)
        out_o[...] = piece[:, wide:].astype(F32)

    pl.when(pl.program_id(0) == 0)(lambda: put(mine[...]))
    pl.when(pl.program_id(0) == 1)(lambda: put(other[...]))


def join_attention(side, mine, other, wh, hd):
    r, n = mine.shape
    place = lambda s, side: jnp.where(s == 0, side[0], 1 - side[0])
    return pl.pallas_call(
        functools.partial(join_attention_kernel, wh),
        grid_spec=pltpu.PrefetchScalarGridSpec(
            num_scalar_prefetch=1,
            grid=(2,),
            in_specs=[pl.BlockSpec((r, n), lambda s, side: (0, 0))] * 2,
            out_specs=[
                pl.BlockSpec((3, r, wh), lambda s, side: (0, place(s, side), 0)),
                pl.BlockSpec((wh, r), lambda s, side: (0, place(s, side))),
                pl.BlockSpec((r, 2 * hd), lambda s, side: (place(s, side), 0)),
            ],
        ),
        out_shape=[
            shape((3, 2 * r, wh), F32), shape((wh, 2 * r), F32), shape((2 * r, 2 * hd), F32),
        ],
        compiler_params=params(32),
        cost_estimate=cost(0, 12 * r * n),
        name="join_attention",
    )(side, mine, other)


def sum_kernel(mid, part_a, part_b, out):
    out[...] = (mid[...] + (part_a[...].astype(F32) + part_b[...].astype(F32))).astype(BF)


def final_sum(mid, part_a, part_b):
    t, d = mid.shape
    return pl.pallas_call(
        sum_kernel,
        grid=(t // BLK,),
        in_specs=[rows(d)] * 3,
        out_specs=rows(d),
        out_shape=shape((t, d), BF),
        compiler_params=params(32),
        cost_estimate=cost(3 * t * d, 8 * MIB),
        name="output_sum",
    )(mid, part_a, part_b)


def per_device(
    n_dp, n_tensor, inputs, seq_lengths, qkv_weight, out_weight, up_weight, down_weight,
    select_weight, norm_gains, grad_output,
):
    wh = qkv_weight.shape[2]
    hd = select_weight.shape[2]
    d = inputs.shape[1]
    sums = Sum(n_dp, n_tensor)
    side = sums.side(0)
    keep_half = side.reshape(1).astype(jnp.int32)
    send_half = 1 - keep_half
    select_t = jnp.swapaxes(select_weight, 1, 2)

    h1, q, k, v, sq, sk, pen, lse, mixed, part = forward(
        seq_lengths, inputs, norm_gains, qkv_weight, select_t, out_weight
    )
    part_other = swap_tensor(part, n_tensor)
    mid, h2, act, du, dn2 = feed(
        inputs, part, part_other, norm_gains, up_weight, down_weight, grad_output
    )
    dn2_other = swap_tensor(dn2, n_tensor)

    down_send = weight_half(send_half, act, grad_output, 256, "grad_down")
    down_keep = weight_half(keep_half, act, grad_output, 256, "grad_down")
    down_piece = sums.scatter(down_send, down_keep)
    up_send = weight_half(send_half, h2, du, 128, "grad_up")
    up_keep = weight_half(keep_half, h2, du, 128, "grad_up")
    up_piece = sums.scatter(up_send, up_keep)

    dmid, gm, dmix, gain_two = middle(mid, dn2, dn2_other, norm_gains, grad_output, out_weight)
    cat = backward(seq_lengths, q, k, v, sq, sk, pen, lse, dmix)
    att_send = attention_weight_half(send_half, h1, cat, mixed, gm)
    att_keep = attention_weight_half(keep_half, h1, cat, mixed, gm)
    att_piece = sums.scatter(att_send, att_keep)

    dn1 = first_grad(cat, qkv_weight, select_t.reshape(2 * hd, d))
    dn1_other = swap_tensor(dn1, n_tensor)
    fold = branch(act, down_weight)
    fold_other = swap_tensor(fold, n_tensor)
    grad_inputs, gain_one = inputs_grad(inputs, dn1, dn1_other, norm_gains, dmid)
    output = final_sum(mid, fold, fold_other)

    gains = jnp.concatenate([gain_one[0:1], gain_two[0:1]], axis=0)
    for stage in range(sums.stages):
        gains = gains + sums.swap(gains, stage)

    grad_down = join(keep_half, *sums.gather(down_piece))
    grad_up = join(keep_half, *sums.gather(up_piece))
    grad_qkv, grad_out, select_part = join_attention(keep_half, *sums.gather(att_piece), wh, hd)
    select_t_sum = select_part.T
    select_t_sum = select_t_sum + swap_tensor(select_t_sum, n_tensor)
    grad_select = jnp.swapaxes(select_t_sum.reshape(2, hd, d), 1, 2)
    return (output, grad_inputs, grad_qkv, grad_out, grad_up, grad_down, grad_select, gains)


def solution(mesh):
    placed = (
        P("dp", None),
        P("dp", None),
        P(None, None, "tensor"),
        P("tensor", None),
        P(None, "tensor"),
        P("tensor", None),
        P(),
        P(),
        P("dp", None),
    )
    return jax.shard_map(
        functools.partial(per_device, mesh.shape["dp"], mesh.shape["tensor"]),
        mesh=mesh,
        in_specs=placed,
        out_specs=(
            P("dp", None),
            P("dp", None),
            P(None, None, "tensor"),
            P("tensor", None),
            P(None, "tensor"),
            P("tensor", None),
            P(),
            P(),
        ),
        check_vma=False,
    )
```

```python
import functools

import jax
import jax.numpy as jnp
from jax import lax
from jax.experimental import pallas as pl
from jax.experimental.pallas import tpu as pltpu
from jax.sharding import PartitionSpec as P

BF = jnp.bfloat16
F32 = jnp.float32
EPS = 1e-6
BLK = 256
NOT_ATTENDED = 1e30
CURVE = 0.7978845608028654
CUBE = 0.044715
MIB = 1024 * 1024
COST = 1.0

DOWN = (0, 1, 2, 3), (1, 2, 0, 3)
UP = (2, 0, 1, 3), (1, 2, 0, 3)
ATT = (0, 1, 2, 3), (2, 0, 1, 3)
EARLY = "d"
LATE = "udnduabduafdugadaugdaugaddaaDuugggAU"
FREE = True


def mm(a, b):
    return jnp.dot(a, b, preferred_element_type=F32)


def mm_nt(a, b):
    return lax.dot_general(a, b, (((1,), (1,)), ((), ())), preferred_element_type=F32)


def mm_tn(a, b):
    return lax.dot_general(a, b, (((0,), (0,)), ((), ())), preferred_element_type=F32)


def params(limit_mib=56):
    return pltpu.CompilerParams(
        dimension_semantics=("arbitrary",), vmem_limit_bytes=limit_mib * MIB
    )


def cost(flops, nbytes, trans=0):
    return pl.CostEstimate(
        flops=int(COST * flops), bytes_accessed=int(COST * nbytes), transcendentals=int(COST * trans)
    )


def shape(dims, dtype):
    return jax.ShapeDtypeStruct(tuple(dims), dtype)


def whole(*dims):
    return pl.BlockSpec(tuple(dims), lambda *_: (0,) * len(dims))


def rows(width, count=BLK):
    return pl.BlockSpec((count, width), lambda i, *_: (i, 0))


def smem():
    return pl.BlockSpec(memory_space=pltpu.SMEM)


def sequence_ids(lens, pos):
    seg = jnp.zeros(pos.shape, jnp.int32)
    first = jnp.zeros(pos.shape, jnp.bool_)
    end = jnp.int32(0)
    for s in range(lens.shape[1]):
        length = lens[0, s]
        first = first | ((pos == end) & (length > 0))
        end = end + length
        seg = seg + (pos >= end).astype(jnp.int32)
    seg = jnp.where(pos < end, seg, lens.shape[1] + 1 + pos)
    return seg, first


def split_dot(values, ones):
    high = values.astype(BF)
    low = (values - high.astype(F32)).astype(BF)
    return mm(high, ones) + mm(low, ones)


def norm_scale(values):
    return lax.rsqrt(jnp.mean(values * values, axis=-1, keepdims=True) + EPS)


def rows_of(i):
    return pl.ds(pl.multiple_of(i * BLK, BLK), BLK)


def triangle(later):
    first = lax.broadcasted_iota(jnp.int32, (BLK, BLK), 0)
    second = lax.broadcasted_iota(jnp.int32, (BLK, BLK), 1)
    return jnp.where(first > second if later else first < second, 1.0, 0.0).astype(BF)


def forward_kernel(
    heads, lens, x, gains, wqkv, wsel_t, wout,
    h1_o, q_o, k_o, v_o, sq_o, sk_o, pen_o, lse_o, mix_o, part_o,
    k_s, vt_s, sk_s, carry_s, qx_s, seg_s, top_s, sum_s, acc_s,
):
    step = pl.program_id(0)
    hd = wsel_t.shape[1]
    t = k_s.shape[0]
    two = 2 * hd
    pairs = heads // 2
    scale = hd**-0.5
    here = rows_of(step)

    @pl.when(step == 0)
    def _():
        carry_s[...] = jnp.zeros_like(carry_s)
        qx_s[...] = jnp.zeros_like(qx_s)
        sk_s[...] = jnp.zeros_like(sk_s)
        seg, first = sequence_ids(lens, lax.broadcasted_iota(jnp.int32, (t, 1), 0))
        seg_s[:, 0:1] = seg
        seg_s[:, 1:2] = jnp.where(first, -1, seg)

    xf = x[...].astype(F32)
    h1 = (xf * norm_scale(xf) * gains[0:1, :]).astype(BF)
    h1_o[...] = h1
    q32 = mm(h1, wqkv[0])
    q = (q32.astype(BF) * scale).astype(BF)
    q_t = (q32.T.astype(BF) * scale).astype(BF)
    k = mm(h1, wqkv[1]).astype(BF)
    v32 = mm(h1, wqkv[2])
    sq = (mm_nt(h1, wsel_t[0]).astype(BF) * scale).astype(BF)
    sk = mm_nt(h1, wsel_t[1]).astype(BF)
    q_o[...] = q
    k_o[...] = k
    v_o[...] = v32.astype(BF)
    sq_o[...] = sq
    sk_o[...] = sk
    k_s[here, :] = k
    sk_s[here, :] = sk
    vt_s[:, here] = v32.T.astype(BF)
    for p in range(pairs):
        for side in range(2):
            h = 2 * p + side
            qx_s[p, side * hd : (side + 1) * hd, side * BLK : (side + 1) * BLK] = q_t[
                h * hd : (h + 1) * hd, :
            ]

    row = step * BLK + lax.broadcasted_iota(jnp.int32, (1, BLK), 1)
    col = lax.broadcasted_iota(jnp.int32, (t, 1), 0)
    seg_i, _ = sequence_ids(lens, row)
    sel = jnp.maximum(mm_nt(sk_s[...], sq), 0.0)
    picked = jnp.where((seg_s[:, 1:2] == seg_i) & (col < row), sel * sel, 0.0)
    pen = split_dot(picked, triangle(False)) + carry_s[:, 0:1]
    carry_s[:, 0:1] = pen[:, BLK - 1 : BLK] + picked[:, BLK - 1 : BLK]
    pen_o[...] = jnp.where((seg_s[:, 0:1] == seg_i) & (col <= row), pen, NOT_ATTENDED)

    top_s[...] = jnp.full_like(top_s, -NOT_ATTENDED)
    sum_s[...] = jnp.zeros_like(sum_s)
    acc_s[...] = jnp.zeros_like(acc_s)

    def tile(j, _):
        at = rows_of(j)
        bias = pen_o[at, :]
        bias = jnp.concatenate([bias, bias], axis=1)
        for p in range(pairs):
            s = mm(k_s[at, p * two : (p + 1) * two], qx_s[p]) - bias
            old = top_s[p : p + 1, :]
            top = jnp.maximum(old, jnp.max(s, axis=0, keepdims=True))
            fade = jnp.exp(old - top)
            prob = jnp.exp(s - top)
            top_s[p : p + 1, :] = top
            sum_s[p : p + 1, :] = sum_s[p : p + 1, :] * fade + jnp.sum(prob, axis=0, keepdims=True)
            low = prob.astype(BF)
            for side in range(2):
                mine = slice((2 * p + side) * hd, (2 * p + side + 1) * hd)
                cut = slice(side * BLK, (side + 1) * BLK)
                acc_s[mine, :] = acc_s[mine, :] * fade[:, cut] + mm(vt_s[mine, at], low[:, cut])
        return 0

    lax.fori_loop(0, step + 1, tile, 0)
    for h in range(heads):
        p, cut = h // 2, slice((h % 2) * BLK, (h % 2 + 1) * BLK)
        total = sum_s[p : p + 1, cut]
        lse_o[h : h + 1, :] = top_s[p : p + 1, cut] + jnp.log(total)
        acc_s[h * hd : (h + 1) * hd, :] = acc_s[h * hd : (h + 1) * hd, :] / total
    mixed = acc_s[...].T.astype(BF)
    mix_o[...] = mixed
    part_o[...] = mm(mixed, wout[...]).astype(BF)


def forward(lens, x, gains, wqkv, wsel_t, wout):
    t, d = x.shape
    wh = wqkv.shape[2]
    hd = wsel_t.shape[1]
    heads = wh // hd
    n = t // BLK
    tall = pl.BlockSpec((t, BLK), lambda i: (0, i))
    return pl.pallas_call(
        functools.partial(forward_kernel, heads),
        grid=(n,),
        in_specs=[
            smem(), rows(d), whole(*gains.shape), whole(*wqkv.shape), whole(*wsel_t.shape),
            whole(*wout.shape),
        ],
        out_specs=[
            rows(d), rows(wh), rows(wh), rows(wh), rows(hd), rows(hd), tall,
            pl.BlockSpec((8, BLK), lambda i: (0, i)), rows(wh), rows(d),
        ],
        out_shape=[
            shape((t, d), BF), shape((t, wh), BF), shape((t, wh), BF), shape((t, wh), BF),
            shape((t, hd), BF), shape((t, hd), BF), shape((t, t), F32), shape((8, t), F32),
            shape((t, wh), BF), shape((t, d), BF),
        ],
        scratch_shapes=[
            pltpu.VMEM((t, wh), BF), pltpu.VMEM((wh, t), BF), pltpu.VMEM((t, hd), BF),
            pltpu.VMEM((t, 128), F32), pltpu.VMEM((heads // 2, 2 * hd, 2 * BLK), BF),
            pltpu.VMEM((t, 128), jnp.int32), pltpu.VMEM((8, 2 * BLK), F32),
            pltpu.VMEM((8, 2 * BLK), F32), pltpu.VMEM((wh, BLK), F32),
        ],
        compiler_params=params(),
        cost_estimate=cost(2 * t * d * (4 * wh + 2 * hd) + 4 * heads * t * t * hd, 16 * MIB, heads * t * t),
        name="attention_forward",
    )(lens, x, gains, wqkv, wsel_t, wout)


def feed_kernel(
    half, x, part_a, part_b, gains, up, down, g, mid_o, h2_o, act_o, du_o, dn_o, dsend_o,
    act_s,
):
    step = pl.program_id(0)
    here = rows_of(step)
    mid = x[...].astype(F32) + (part_a[...].astype(F32) + part_b[...].astype(F32))
    mid_o[...] = mid
    h2 = (mid * norm_scale(mid) * gains[1:2, :]).astype(BF)
    h2_o[...] = h2
    hidden = up.shape[1]
    chunk = 512
    dn = jnp.zeros(mid.shape, F32)
    for c in range(hidden // chunk):
        cut = slice(c * chunk, (c + 1) * chunk)
        u = mm(h2, up[:, cut])
        da = mm_nt(g[here, :], down[cut, :])
        u2 = u * u
        curve = jnp.tanh(u * (CURVE + (CURVE * CUBE) * u2))
        part = 0.5 * (1.0 + curve)
        act = (u * part).astype(BF)
        slope = part + (0.5 * u) * (1.0 - curve * curve) * (CURVE + (3.0 * CURVE * CUBE) * u2)
        du = (da * slope).astype(BF)
        act_o[:, cut] = act
        act_s[here, cut] = act
        du_o[:, cut] = du
        dn = dn + mm_nt(du, up[:, cut])
    dn_o[...] = dn.astype(BF)

    @pl.when(step == pl.num_programs(0) - 1)
    def _():
        tile = 128
        for j in range(dsend_o.shape[0] // tile):
            at = pl.ds(pl.multiple_of(half[0] * dsend_o.shape[0] + j * tile, tile), tile)
            dsend_o[j * tile : (j + 1) * tile, :] = mm_tn(act_s[:, at], g[...]).astype(BF)


def feed(half, x, part_a, part_b, gains, up, down, g):
    t, d = x.shape
    hidden = up.shape[1]
    return pl.pallas_call(
        feed_kernel,
        grid=(t // BLK,),
        in_specs=[
            smem(), rows(d), rows(d), rows(d), whole(*gains.shape), whole(*up.shape),
            whole(*down.shape), whole(t, d),
        ],
        out_specs=[
            rows(d), rows(d), rows(hidden), rows(hidden), rows(d), whole(hidden // 2, d),
        ],
        out_shape=[
            shape((t, d), F32), shape((t, d), BF), shape((t, hidden), BF), shape((t, hidden), BF),
            shape((t, d), BF), shape((hidden // 2, d), BF),
        ],
        scratch_shapes=[pltpu.VMEM((t, hidden), BF)],
        compiler_params=params(),
        cost_estimate=cost(8 * t * d * hidden, 24 * MIB, t * hidden),
        name="feed_forward",
    )(half, x, part_a, part_b, gains, up, down, g)


def product_kernel(half, left, right, out):
    out[...] = mm_tn(left[...], right[...]).astype(BF)


def down_half(half, act, g):
    t, hidden = act.shape
    d = g.shape[1]
    tiles = 3
    tile = hidden // 2 // tiles
    return pl.pallas_call(
        product_kernel,
        grid_spec=pltpu.PrefetchScalarGridSpec(
            num_scalar_prefetch=1,
            grid=(tiles,),
            in_specs=[
                pl.BlockSpec((t, tile), lambda j, half: (0, half[0] * tiles + j)),
                whole(t, d),
            ],
            out_specs=pl.BlockSpec((tile, d), lambda j, half: (j, 0)),
        ),
        out_shape=shape((hidden // 2, d), BF),
        compiler_params=params(),
        cost_estimate=cost(t * d * hidden, 6 * MIB),
        name="grad_down",
    )(half, act, g)


def norm_back(values, scale, gain, grad):
    unit = values * scale
    grad_unit = grad * gain
    mean = jnp.mean(grad_unit * unit, axis=-1, keepdims=True)
    return scale * (grad_unit - unit * mean), jnp.sum(grad * unit, axis=0, keepdims=True)


def middle_kernel(
    hd, half, mid, part_a, part_b, gains, g, wout, mixed, h2, du, dmid_o, gm_o, dmix_o, dots_o,
    send_o, keep_o, gain_o, gm_s,
):
    step = pl.program_id(0)
    here = rows_of(step)
    values = mid[...]
    grad = part_a[...].astype(F32) + part_b[...].astype(F32)
    back, gain_grad = norm_back(values, norm_scale(values), gains[1:2, :], grad)
    dmid = g[...].astype(F32) + back
    dmid_o[...] = dmid
    gm = dmid.astype(BF)
    gm_o[...] = gm
    gm_s[here, :] = gm
    dmix = mm_nt(gm, wout[...]).astype(BF)
    dmix_o[...] = dmix
    both = (dmix.astype(F32) * mixed[here, :].astype(F32)).T
    for h in range(both.shape[0] // hd):
        dots_o[h : h + 1, :] = jnp.sum(both[h * hd : (h + 1) * hd, :], axis=0, keepdims=True)

    @pl.when(step == 0)
    def _():
        gain_o[...] = jnp.zeros_like(gain_o)

    gain_o[0:1, :] += gain_grad

    @pl.when(step == pl.num_programs(0) - 1)
    def _():
        hidden = du.shape[1]
        size = send_o.shape[0]
        tile = 128
        for which, into in ((half[0], send_o), (1 - half[0], keep_o)):
            half_at = pl.multiple_of(which * size, tile)
            for r in range(size // tile):
                out = slice(r * tile, (r + 1) * tile)
                at = pl.ds(pl.multiple_of(half_at + r * tile, tile), tile)
                into[out, :hidden] = mm_tn(h2[:, at], du[...]).astype(BF)
                into[out, hidden:] = mm_tn(mixed[:, out], gm_s[:, pl.ds(half_at, size)]).astype(BF)


def middle(half, mid, part_a, part_b, gains, g, wout, mixed, h2, du, hd):
    t, d = mid.shape
    wh = wout.shape[0]
    hidden = du.shape[1]
    return pl.pallas_call(
        functools.partial(middle_kernel, hd),
        grid=(t // BLK,),
        in_specs=[
            smem(), rows(d), rows(d), rows(d), whole(*gains.shape), rows(d), whole(*wout.shape),
            whole(t, wh), whole(t, d), whole(t, hidden),
        ],
        out_specs=[
            rows(d), rows(d), rows(wh), pl.BlockSpec((8, BLK), lambda i: (0, i)),
            whole(d // 2, hidden + d // 2), whole(d // 2, hidden + d // 2), whole(8, d),
        ],
        out_shape=[
            shape((t, d), F32), shape((t, d), BF), shape((t, wh), BF), shape((8, t), F32),
            shape((d // 2, hidden + d // 2), BF), shape((d // 2, hidden + d // 2), BF),
            shape((8, d), F32),
        ],
        scratch_shapes=[pltpu.VMEM((t, d), BF)],
        compiler_params=params(),
        cost_estimate=cost(2 * t * d * wh + t * d * hidden, 20 * MIB),
        name="second_norm_backward",
    )(half, mid, part_a, part_b, gains, g, wout, mixed, h2, du)


def split_three(values):
    one = values.astype(BF).astype(F32)
    rest = values - one
    two = rest.astype(BF).astype(F32)
    return one, two, (rest - two).astype(BF).astype(F32)


def backward_kernel(
    n_blocks, heads, lens, half, q, k, v, sq, sk, pen, lse, dots, dmix, h1, cat_o, send_o, keep_o,
    qx_s, qm_s, dx_s, dm_s, dq_s, dsq_s, dk_s, dv_s, dsk_s, kt_s, skt_s, kx_s, vx_s, seg_s,
):
    j = pl.program_id(0)
    wh = k.shape[1]
    hd = sk.shape[1]
    t = q.shape[0]
    two = 2 * hd
    pairs = heads // 2
    scale = hd**-0.5
    lane = lax.broadcasted_iota(jnp.int32, (1, two), 1)
    side_of = [lane // hd == side for side in range(2)]
    ones = jnp.broadcast_to(jnp.where(lane < 3, 1.0, 0.0).astype(BF), (BLK, two))

    @pl.when(j == 0)
    def _():
        dq_s[...] = jnp.zeros_like(dq_s)
        dsq_s[...] = jnp.zeros_like(dsq_s)
        seg, _ = sequence_ids(lens, lax.broadcasted_iota(jnp.int32, (1, t), 1))
        seg_s[0:1, :] = seg

        tall = lax.broadcasted_iota(jnp.int32, (two, 1), 0)

        def prepare(i, _):
            at = rows_of(i)
            for which, (source, plain, wide) in enumerate(((q, qm_s, qx_s), (dmix, dm_s, dx_s))):
                source_t = source[at, :].astype(F32).T
                for h in range(heads):
                    side = h % 2
                    pair = slice((h // 2) * two, (h // 2 + 1) * two)
                    cut = slice(side * BLK, (side + 1) * BLK)
                    value = jnp.where(side_of[side], source[at, pair], jnp.zeros((), BF))
                    plain[h // 2, i, cut, :] = value
                    value = jnp.where(tall // hd == side, source_t[pair, :], 0.0)
                    wide[h // 2, i, 0:two, cut] = value.astype(BF)
                    one, mid, low = split_three(-(lse, dots)[which][h : h + 1, at])
                    value = jnp.where(tall == 0, one, jnp.where(tall == 1, mid, jnp.where(tall == 2, low, 0.0)))
                    wide[h // 2, i, two : 2 * two, cut] = value.astype(BF)
            return 0

        lax.fori_loop(0, n_blocks, prepare, 0)

    here = rows_of(j)
    dk_s[...] = jnp.zeros_like(dk_s)
    dv_s[...] = jnp.zeros_like(dv_s)
    dsk_s[...] = jnp.zeros_like(dsk_s)
    kt_s[...] = k[...].astype(F32).T.astype(BF)
    skt_s[...] = sk[...].astype(F32).T.astype(BF)
    for p in range(pairs):
        pair = slice(p * two, (p + 1) * two)
        kx_s[p, :, 0:two] = k[:, pair]
        vx_s[p, :, 0:two] = v[:, pair]
        kx_s[p, :, two:] = ones
        vx_s[p, :, two:] = ones
    after = triangle(True)
    col = j * BLK + lax.broadcasted_iota(jnp.int32, (BLK, 1), 0)
    seg_j, first_j = sequence_ids(lens, col)
    seg_j = jnp.where(first_j, -1, seg_j)

    def tile(back, carry):
        i = n_blocks - 1 - back
        at = rows_of(i)
        bias = pen[:, at]
        dpen = None
        for p in range(pairs):
            pair = slice(p * two, (p + 1) * two)
            prob = jnp.exp(mm(kx_s[p], qx_s[p, i]) - jnp.concatenate([bias, bias], axis=1))
            dscore = prob * mm(vx_s[p], dx_s[p, i])
            both = dscore[:, :BLK] + dscore[:, BLK:]
            dpen = both if dpen is None else dpen + both
            low = dscore.astype(BF)
            for side in range(2):
                h = 2 * p + side
                dq_s[p, side * hd : (side + 1) * hd, at] += mm(
                    kt_s[h * hd : (h + 1) * hd, :], low[:, side * BLK : (side + 1) * BLK]
                )
            dv_s[:, pair] += mm(prob.astype(BF), dm_s[p, i])
            dk_s[:, pair] += mm(low, qm_s[p, i])
        dpicked = split_dot(dpen, after) + carry
        row = i * BLK + lax.broadcasted_iota(jnp.int32, (1, BLK), 1)
        chosen = (seg_j == seg_s[0:1, at]) & (col < row)
        sel = jnp.maximum(mm_nt(sk[...], sq[at, :]), 0.0)
        dsel = jnp.where(chosen, -2.0 * dpicked * sel, 0.0).astype(BF)
        dsk_s[...] += mm(dsel, sq[at, :])
        dsq_s[:, at] += mm(skt_s[...], dsel)
        return dpicked[:, 0:1] + dpen[:, 0:1]

    lax.fori_loop(0, n_blocks - j, tile, jnp.zeros((BLK, 1), F32))
    cat_o[here, wh : 2 * wh] = dk_s[...].astype(BF)
    cat_o[here, 2 * wh : 3 * wh] = dv_s[...].astype(BF)
    cat_o[here, 3 * wh + hd : 3 * wh + 2 * hd] = dsk_s[...].astype(BF)

    @pl.when(j == n_blocks - 1)
    def _():
        for p in range(pairs):
            cat_o[:, p * two : (p + 1) * two] = (dq_s[p] * scale).T.astype(BF)
        cat_o[:, 3 * wh : 3 * wh + hd] = (dsq_s[...] * scale).T.astype(BF)
        size = send_o.shape[0]
        tile = 128
        for which, into in ((half[0], send_o), (1 - half[0], keep_o)):
            for r in range(size // tile):
                at = pl.ds(pl.multiple_of(which * size + r * tile, tile), tile)
                into[r * tile : (r + 1) * tile, :] = mm_tn(h1[:, at], cat_o[...]).astype(BF)


def backward(lens, half, q, k, v, sq, sk, pen, lse, dots, dmix, h1):
    d = h1.shape[1]
    t, wh = q.shape
    hd = sq.shape[1]
    heads = wh // hd
    n = t // BLK
    width = 3 * wh + 2 * hd
    per_head = pltpu.VMEM((heads // 2, n, 2 * BLK, 2 * hd), BF)
    per_head_t = pltpu.VMEM((heads // 2, n, 4 * hd, 2 * BLK), BF)
    return pl.pallas_call(
        functools.partial(backward_kernel, n, heads),
        grid=(n,),
        in_specs=[
            smem(), smem(), whole(t, wh), rows(wh), rows(wh), whole(t, hd), rows(hd), rows(t),
            whole(8, t), whole(8, t), whole(t, wh), whole(t, d),
        ],
        out_specs=[whole(t, width), whole(d // 2, width), whole(d // 2, width)],
        out_shape=[
            shape((t, width), BF), shape((d // 2, width), BF), shape((d // 2, width), BF),
        ],
        scratch_shapes=[
            per_head_t, per_head, per_head_t, per_head, pltpu.VMEM((heads // 2, 2 * hd, t), F32),
            pltpu.VMEM((hd, t), F32), pltpu.VMEM((BLK, wh), F32),
            pltpu.VMEM((BLK, wh), F32), pltpu.VMEM((BLK, hd), F32), pltpu.VMEM((wh, BLK), BF),
            pltpu.VMEM((hd, BLK), BF), pltpu.VMEM((heads // 2, BLK, 4 * hd), BF),
            pltpu.VMEM((heads // 2, BLK, 4 * hd), BF), pltpu.VMEM((8, t), jnp.int32),
        ],
        compiler_params=params(),
        cost_estimate=cost(10 * heads * t * t * hd, 12 * MIB, heads * t * t),
        name="attention_backward",
    )(lens, half, q, k, v, sq, sk, pen, lse, dots, dmix, h1)


def first_kernel(cat, wqkv, wsel, out):
    wh = wqkv.shape[2]
    total = mm(cat[:, 3 * wh :], wsel[...])
    for i in range(3):
        total = total + mm_nt(cat[:, i * wh : (i + 1) * wh], wqkv[i])
    out[...] = total.astype(BF)


def first_grad(cat, wqkv, wsel):
    t, width = cat.shape
    d = wqkv.shape[1]
    return pl.pallas_call(
        first_kernel,
        grid=(t // BLK,),
        in_specs=[rows(width), whole(*wqkv.shape), whole(*wsel.shape)],
        out_specs=rows(d),
        out_shape=shape((t, d), BF),
        compiler_params=params(),
        cost_estimate=cost(2 * t * d * width, 6 * MIB),
        name="first_norm_grad",
    )(cat, wqkv, wsel)


def finish_kernel(
    x, part_a, part_b, gains, dmid, mid, fold_a, fold_b, grad_o, out_o, gain_o
):
    values = x[...].astype(F32)
    grad = part_a[...].astype(F32) + part_b[...].astype(F32)
    back, gain_grad = norm_back(values, norm_scale(values), gains[0:1, :], grad)
    grad_o[...] = dmid[...] + back
    out_o[...] = (mid[...] + (fold_a[...].astype(F32) + fold_b[...].astype(F32))).astype(BF)

    @pl.when(pl.program_id(0) == 0)
    def _():
        gain_o[...] = jnp.zeros_like(gain_o)

    gain_o[0:1, :] += gain_grad


def finish(x, part_a, part_b, gains, dmid, mid, fold_a, fold_b):
    t, d = x.shape
    return pl.pallas_call(
        finish_kernel,
        grid=(t // BLK,),
        in_specs=[rows(d), rows(d), rows(d), whole(*gains.shape)] + [rows(d)] * 4,
        out_specs=[rows(d), rows(d), whole(8, d)],
        out_shape=[shape((t, d), F32), shape((t, d), BF), shape((8, d), F32)],
        compiler_params=params(),
        cost_estimate=cost(24 * t * d, 20 * MIB),
        name="first_norm_backward",
    )(x, part_a, part_b, gains, dmid, mid, fold_a, fold_b)


def branch_kernel(act, down, out):
    out[...] = mm(act[...], down[...]).astype(BF)


def branch(act, down):
    t, hidden = act.shape
    d = down.shape[1]
    return pl.pallas_call(
        branch_kernel,
        grid=(t // BLK,),
        in_specs=[rows(hidden), whole(*down.shape)],
        out_specs=rows(d),
        out_shape=shape((t, d), BF),
        compiler_params=params(),
        cost_estimate=cost(2 * t * d * hidden, 8 * MIB),
        name="down_projection",
    )(act, down)


class Sum:
    def __init__(self, n_dp, n_tensor, orders):
        self.n_dp, self.n_tensor = n_dp, n_tensor
        self.stages = n_dp.bit_length() - 1
        rest = list(range(4, self.stages))
        self.orders = [[1 << b for b in list(orders[t % 2]) + rest] for t in range(n_tensor)]
        self.dp = lax.axis_index("dp")
        self.tensor = lax.axis_index("tensor")

    def place(self, stage):
        out = (self.dp // self.orders[0][stage]) % 2
        for t in range(1, self.n_tensor):
            out = jnp.where(self.tensor == t, (self.dp // self.orders[t][stage]) % 2, out)
        return out

    def swap(self, value, stage):
        pairs = [
            (i * self.n_tensor + t, (i ^ self.orders[t][stage]) * self.n_tensor + t)
            for i in range(self.n_dp)
            for t in range(self.n_tensor)
        ]
        return lax.ppermute(value, ("dp", "tensor"), pairs)

    def split(self, stage, *terms):
        size = terms[0].shape[0] // 2
        place = self.place(stage)

        def cut(which):
            pieces = [lax.dynamic_slice_in_dim(v, which * size, size, 0) for v in terms]
            return (pieces[0].astype(F32) + pieces[1].astype(F32)).astype(BF)

        return [cut(1 - place), cut(place)]

    def join(self, stage, mine, other):
        place = self.place(stage)
        low, high = jnp.where(place == 0, mine, other), jnp.where(place == 0, other, mine)
        return jnp.concatenate([low, high], axis=0)


class Chain:
    def __init__(self, sums, line):
        self.sums, self.line, self.stage = sums, line, 0

    def begin(self, send):
        self.got = self.sums.swap(send, 0)

    def hold(self, keep):
        self.keep = keep

    def reduce(self):
        sums, self.stage = self.sums, self.stage + 1
        if self.stage < sums.stages:
            split = functools.partial(sums.split, self.stage)
            send, self.keep = self.line.run(split, self.keep, self.got)
            self.got = sums.swap(send, self.stage)
        else:
            add = lambda a, b: [(a.astype(F32) + b.astype(F32)).astype(BF)]
            (self.piece,) = self.line.run(add, self.keep, self.got)
            self.spread()

    def spread(self):
        self.stage -= 1
        self.got = self.sums.swap(self.piece, self.stage)

    def gather(self):
        join = lambda *v: [self.sums.join(self.stage, *v)]
        (self.piece,) = self.line.run(join, self.piece, self.got)
        self.spread()

    def step(self):
        if not hasattr(self, "piece"):
            self.reduce()
        elif self.stage > 0:
            self.gather()
        else:
            return False
        return True

    def halves(self):
        return self.piece, self.got


class Line:
    def __init__(self):
        self.token = None

    def run(self, step, *values, after=()):
        if self.token is not None:
            first, *_ = lax.optimization_barrier((values[0], self.token, *after))
            values = (first, *values[1:])
        out = step(*values)
        self.token = out[0]
        return out


def swap_tensor(value, n_tensor):
    return lax.ppermute(value, "tensor", [(t, t ^ 1) for t in range(n_tensor)])


def join_kernel(side, mine, other, out):
    @pl.when(pl.program_id(0) == 0)
    def _():
        out[...] = mine[...].astype(F32)

    @pl.when(pl.program_id(0) == 1)
    def _():
        out[...] = other[...].astype(F32)


def join(side, mine, other):
    r, n = mine.shape
    tiles = 3
    tile = r // tiles
    return pl.pallas_call(
        join_kernel,
        grid_spec=pltpu.PrefetchScalarGridSpec(
            num_scalar_prefetch=1,
            grid=(2, tiles),
            in_specs=[
                pl.BlockSpec((tile, n), lambda s, j, side: (jnp.where(s == 0, j, tiles - 1), 0)),
                pl.BlockSpec((tile, n), lambda s, j, side: (jnp.where(s == 0, 0, j), 0)),
            ],
            out_specs=pl.BlockSpec(
                (tile, n), lambda s, j, side: (jnp.where(s == 0, side[0], 1 - side[0]) * tiles + j, 0)
            ),
        ),
        out_shape=shape((2 * r, n), F32),
        compiler_params=pltpu.CompilerParams(
            dimension_semantics=("arbitrary", "arbitrary"), vmem_limit_bytes=32 * MIB
        ),
        cost_estimate=cost(0, 12 * r * n),
        name="join_halves",
    )(side, mine, other)


def join_up_kernel(side, mine, other, up_o, out_o):
    def put(piece):
        up_o[...] = piece[:, : up_o.shape[1]].astype(F32)
        out_o[...] = piece[:, up_o.shape[1] :].astype(F32)

    pl.when(pl.program_id(0) == 0)(lambda: put(mine[...]))
    pl.when(pl.program_id(0) == 1)(lambda: put(other[...]))


def join_up(side, mine, other, hidden, wh):
    r, n = mine.shape
    place = lambda s, side: jnp.where(s == 0, side[0], 1 - side[0])
    return pl.pallas_call(
        join_up_kernel,
        grid_spec=pltpu.PrefetchScalarGridSpec(
            num_scalar_prefetch=1,
            grid=(2,),
            in_specs=[pl.BlockSpec((r, n), lambda s, side: (0, 0))] * 2,
            out_specs=[
                pl.BlockSpec((r, hidden), lambda s, side: (place(s, side), 0)),
                pl.BlockSpec((wh, r), lambda s, side: (0, place(s, side))),
            ],
        ),
        out_shape=[shape((2 * r, hidden), F32), shape((wh, 2 * r), F32)],
        compiler_params=params(32),
        cost_estimate=cost(0, 12 * r * n),
        name="join_up",
    )(side, mine, other)


def join_attention_kernel(wh, side, mine, other, qkv_o, sel_o):
    def put(piece):
        for i in range(3):
            qkv_o[i] = piece[:, i * wh : (i + 1) * wh].astype(F32)
        sel_o[...] = piece[:, 3 * wh :].astype(F32)

    pl.when(pl.program_id(0) == 0)(lambda: put(mine[...]))
    pl.when(pl.program_id(0) == 1)(lambda: put(other[...]))


def join_attention(side, mine, other, wh, hd):
    r, n = mine.shape
    place = lambda s, side: jnp.where(s == 0, side[0], 1 - side[0])
    return pl.pallas_call(
        functools.partial(join_attention_kernel, wh),
        grid_spec=pltpu.PrefetchScalarGridSpec(
            num_scalar_prefetch=1,
            grid=(2,),
            in_specs=[pl.BlockSpec((r, n), lambda s, side: (0, 0))] * 2,
            out_specs=[
                pl.BlockSpec((3, r, wh), lambda s, side: (0, place(s, side), 0)),
                pl.BlockSpec((r, 2 * hd), lambda s, side: (place(s, side), 0)),
            ],
        ),
        out_shape=[shape((3, 2 * r, wh), F32), shape((2 * r, 2 * hd), F32)],
        compiler_params=params(32),
        cost_estimate=cost(0, 12 * r * n),
        name="join_attention",
    )(side, mine, other)


def per_device(
    n_dp, n_tensor, inputs, seq_lengths, qkv_weight, out_weight, up_weight, down_weight,
    select_weight, norm_gains, grad_output,
):
    wh = qkv_weight.shape[2]
    hd = select_weight.shape[2]
    d = inputs.shape[1]
    hidden = up_weight.shape[1]
    line = Line()
    run = line.run
    sums = [Sum(n_dp, n_tensor, orders) for orders in (DOWN, UP, ATT)]
    down, up, att = (Chain(each, line) for each in sums)
    small = sums[0]
    down_kept, up_kept, att_kept = (
        each.place(0).reshape(1).astype(jnp.int32) for each in sums
    )
    select_t = jnp.swapaxes(select_weight, 1, 2)
    swap = functools.partial(swap_tensor, n_tensor=n_tensor)

    h1, q, k, v, sq, sk, pen, lse, mixed, part = run(
        forward, seq_lengths, inputs, norm_gains, qkv_weight, select_t, out_weight
    )
    mid, h2, act, du, dn2, down_send = run(
        lambda part, *v: feed(1 - down_kept, inputs, part, *v),
        part, swap(part), norm_gains, up_weight, down_weight, grad_output,
    )
    dn2_other = swap(dn2)
    down.begin(down_send)
    down.hold(*run(lambda act, *v: [down_half(down_kept, act, *v)], act, grad_output))
    dmid, gm, dmix, dots, up_send, up_keep, gain_two = run(
        lambda dn2, *v: middle(1 - up_kept, mid, dn2, *v, hd),
        dn2, dn2_other, norm_gains, grad_output, out_weight, mixed, h2, du,
    )
    up.begin(up_send)
    up.hold(up_keep)
    steps = {"d": down.step, "u": up.step, "a": att.step}
    for letter in EARLY:
        steps[letter]()
    cat, att_send, att_keep = run(
        lambda dots, *v: backward(seq_lengths, 1 - att_kept, *v[:7], dots, *v[7:]),
        dots, q, k, v, sq, sk, pen, lse, dmix, h1,
    )
    att.begin(att_send)
    att.hold(att_keep)
    done = {}

    def first():
        value = (first_grad if FREE else over(first_grad))(cat, qkv_weight, select_t.reshape(2 * hd, d))
        done["dn1"] = value, swap(value)

    def fold():
        value = (branch if FREE else over(branch))(act, down_weight)
        done["fold"] = value, swap(value)

    def over(kernel):
        return lambda *v: run(lambda *w: [kernel(*w)], *v)[0]

    def last():
        done["inputs"], done["output"], gain_one = run(
            lambda dn1, *v: finish(inputs, dn1, *v),
            *done["dn1"], norm_gains, dmid, mid, *done["fold"],
        )
        done["gains"] = jnp.concatenate([gain_one[0:1], gain_two[0:1]], axis=0), 0

    def gain():
        value, stage = done["gains"]
        if stage == small.stages:
            return False
        (value,) = run(lambda *v: [v[0] + v[1]], value, small.swap(value, stage))
        done["gains"] = value, stage + 1
        return True

    def down_out():
        while down.step():
            pass
        (done["down"],) = run(lambda *v: [join(down_kept, *v)], *down.halves())

    def up_out():
        while up.step():
            pass
        done["up"] = run(lambda *v: join_up(up_kept, *v, hidden, wh), *up.halves())

    def att_out():
        while att.step():
            pass
        done["att"] = run(lambda *v: join_attention(att_kept, *v, wh, hd), *att.halves())

    steps.update(n=first, b=fold, f=last, g=gain, D=down_out, U=up_out, A=att_out)
    for letter in LATE:
        steps[letter]()
    while gain():
        pass
    grad_inputs, output, gains, grad_down = (done[k] for k in ("inputs", "output", "gains", "down"))
    gains = gains[0]
    grad_up, grad_out = done["up"]
    grad_qkv, select_part = done["att"]
    select_t_sum = select_part.T
    select_t_sum = select_t_sum + swap(select_t_sum)
    grad_select = jnp.swapaxes(select_t_sum.reshape(2, hd, d), 1, 2)
    return (output, grad_inputs, grad_qkv, grad_out, grad_up, grad_down, grad_select, gains)


def solution(mesh):
    placed = (
        P("dp", None),
        P("dp", None),
        P(None, None, "tensor"),
        P("tensor", None),
        P(None, "tensor"),
        P("tensor", None),
        P(),
        P(),
        P("dp", None),
    )
    return jax.shard_map(
        functools.partial(per_device, mesh.shape["dp"], mesh.shape["tensor"]),
        mesh=mesh,
        in_specs=placed,
        out_specs=(
            P("dp", None),
            P("dp", None),
            P(None, None, "tensor"),
            P("tensor", None),
            P(None, "tensor"),
            P("tensor", None),
            P(),
            P(),
        ),
        check_vma=False,
    )
```

```python
import functools

import jax
import jax.numpy as jnp
from jax import lax
from jax.experimental import pallas as pl
from jax.experimental.pallas import tpu as pltpu
from jax.sharding import PartitionSpec as P

BF = jnp.bfloat16
F32 = jnp.float32
EPS = 1e-6
BLK = 256
NOT_ATTENDED = 1e30
CURVE = 0.7978845608028654
CUBE = 0.044715
MIB = 1024 * 1024
COST = 1.0

DOWN = (0, 1, 2, 3), (1, 2, 0, 3)
UP = (2, 0, 1, 3), (1, 2, 0, 3)
ATT = (0, 1, 2, 3), (2, 0, 1, 3)
EARLY = "d"
LATE = "dbudnudaufuadaudaugaddugaagdDagAgguU"
FREE = False

SHARES = (3.0, 3.0, 3.0, 3.0, 3.0, 3.0)


def mm(a, b):
    return jnp.dot(a, b, preferred_element_type=F32)


def mm_nt(a, b):
    return lax.dot_general(a, b, (((1,), (1,)), ((), ())), preferred_element_type=F32)


def mm_tn(a, b):
    return lax.dot_general(a, b, (((0,), (0,)), ((), ())), preferred_element_type=F32)


def params(limit_mib=56):
    return pltpu.CompilerParams(
        dimension_semantics=("arbitrary",), vmem_limit_bytes=limit_mib * MIB
    )


def cost(flops, nbytes, trans=0, share=1.0):
    return pl.CostEstimate(
        flops=int(COST * share * flops), bytes_accessed=int(COST * share * nbytes),
        transcendentals=int(COST * share * trans),
    )


def shape(dims, dtype):
    return jax.ShapeDtypeStruct(tuple(dims), dtype)


def whole(*dims):
    return pl.BlockSpec(tuple(dims), lambda *_: (0,) * len(dims))


def rows(width, count=BLK):
    return pl.BlockSpec((count, width), lambda i, *_: (i, 0))


def anywhere():
    return pl.BlockSpec(memory_space=pl.ANY)


def fetch(start, wait, *copies):
    for condition, act in ((start, "start"), (wait, "wait")):
        if condition is None:
            continue

        @pl.when(condition)
        def _():
            for copy in copies:
                getattr(pltpu.make_async_copy(*copy), act)()


def smem():
    return pl.BlockSpec(memory_space=pltpu.SMEM)


def sequence_ids(lens, pos):
    seg = jnp.zeros(pos.shape, jnp.int32)
    first = jnp.zeros(pos.shape, jnp.bool_)
    end = jnp.int32(0)
    for s in range(lens.shape[1]):
        length = lens[0, s]
        first = first | ((pos == end) & (length > 0))
        end = end + length
        seg = seg + (pos >= end).astype(jnp.int32)
    seg = jnp.where(pos < end, seg, lens.shape[1] + 1 + pos)
    return seg, first


def split_dot(values, ones):
    high = values.astype(BF)
    low = (values - high.astype(F32)).astype(BF)
    return mm(high, ones) + mm(low, ones)


def norm_scale(values):
    return lax.rsqrt(jnp.mean(values * values, axis=-1, keepdims=True) + EPS)


def rows_of(i):
    return pl.ds(pl.multiple_of(i * BLK, BLK), BLK)


def triangle(later):
    first = lax.broadcasted_iota(jnp.int32, (BLK, BLK), 0)
    second = lax.broadcasted_iota(jnp.int32, (BLK, BLK), 1)
    return jnp.where(first > second if later else first < second, 1.0, 0.0).astype(BF)


def forward_kernel(
    heads, lens, x, gains, wqkv, wsel_t, wout,
    h1_o, q_o, k_o, v_o, sq_o, sk_o, pen_o, lse_o, mix_o, part_o,
    k_s, vt_s, sk_s, carry_s, qx_s, seg_s, top_s, sum_s, acc_s,
):
    step = pl.program_id(0)
    hd = wsel_t.shape[1]
    t = k_s.shape[0]
    two = 2 * hd
    pairs = heads // 2
    scale = hd**-0.5
    here = rows_of(step)

    @pl.when(step == 0)
    def _():
        carry_s[...] = jnp.zeros_like(carry_s)
        qx_s[...] = jnp.zeros_like(qx_s)
        seg, first = sequence_ids(lens, lax.broadcasted_iota(jnp.int32, (t, 1), 0))
        seg_s[:, 0:1] = seg
        seg_s[:, 1:2] = jnp.where(first, -1, seg)

    xf = x[...].astype(F32)
    h1 = (xf * norm_scale(xf) * gains[0:1, :]).astype(BF)
    h1_o[...] = h1
    q32 = mm(h1, wqkv[0])
    q = (q32.astype(BF) * scale).astype(BF)
    q_t = (q32.T.astype(BF) * scale).astype(BF)
    k = mm(h1, wqkv[1]).astype(BF)
    v32 = mm(h1, wqkv[2])
    sq = (mm_nt(h1, wsel_t[0]).astype(BF) * scale).astype(BF)
    sk = mm_nt(h1, wsel_t[1]).astype(BF)
    q_o[...] = q
    k_o[...] = k
    v_o[...] = v32.astype(BF)
    sq_o[...] = sq
    sk_o[...] = sk
    k_s[here, :] = k
    sk_s[here, :] = sk
    vt_s[:, here] = v32.T.astype(BF)
    for p in range(pairs):
        for side in range(2):
            h = 2 * p + side
            qx_s[p, side * hd : (side + 1) * hd, side * BLK : (side + 1) * BLK] = q_t[
                h * hd : (h + 1) * hd, :
            ]

    row = step * BLK + lax.broadcasted_iota(jnp.int32, (1, BLK), 1)
    seg_i, _ = sequence_ids(lens, row)
    before = triangle(False)
    top_s[...] = jnp.full_like(top_s, -NOT_ATTENDED)
    sum_s[...] = jnp.zeros_like(sum_s)
    acc_s[...] = jnp.zeros_like(acc_s)

    def tile(j, _):
        at = rows_of(j)
        raw = [mm(k_s[at, p * two : (p + 1) * two], qx_s[p]) for p in range(pairs)]
        col = j * BLK + lax.broadcasted_iota(jnp.int32, (BLK, 1), 0)
        sel = jnp.maximum(mm_nt(sk_s[at, :], sq), 0.0)
        picked = jnp.where((seg_s[at, 1:2] == seg_i) & (col < row), sel * sel, 0.0)
        pen = split_dot(picked, before) + carry_s[at, 0:1]
        carry_s[at, 0:1] = pen[:, BLK - 1 : BLK] + picked[:, BLK - 1 : BLK]
        bias = jnp.where((seg_s[at, 0:1] == seg_i) & (col <= row), pen, NOT_ATTENDED)
        pen_o[at, :] = bias
        bias = jnp.concatenate([bias, bias], axis=1)
        lows, fades = [], []
        for p in range(pairs):
            s = raw[p] - bias
            old = top_s[p : p + 1, :]
            top = jnp.maximum(old, jnp.max(s, axis=0, keepdims=True))
            fade = jnp.exp(old - top)
            prob = jnp.exp(s - top)
            top_s[p : p + 1, :] = top
            sum_s[p : p + 1, :] = sum_s[p : p + 1, :] * fade + jnp.sum(prob, axis=0, keepdims=True)
            lows.append(prob.astype(BF))
            fades.append(fade)
        for h in range(heads):
            p, cut = h // 2, slice((h % 2) * BLK, (h % 2 + 1) * BLK)
            mine = slice(h * hd, (h + 1) * hd)
            acc_s[mine, :] = acc_s[mine, :] * fades[p][:, cut] + mm(vt_s[mine, at], lows[p][:, cut])
        return 0

    lax.fori_loop(0, step + 1, tile, 0)
    for h in range(heads):
        p, cut = h // 2, slice((h % 2) * BLK, (h % 2 + 1) * BLK)
        total = sum_s[p : p + 1, cut]
        lse_o[h : h + 1, :] = top_s[p : p + 1, cut] + jnp.log(total)
        acc_s[h * hd : (h + 1) * hd, :] = acc_s[h * hd : (h + 1) * hd, :] / total
    mixed = acc_s[...].T.astype(BF)
    mix_o[...] = mixed
    part_o[...] = mm(mixed, wout[...]).astype(BF)


def forward(lens, x, gains, wqkv, wsel_t, wout):
    t, d = x.shape
    wh = wqkv.shape[2]
    hd = wsel_t.shape[1]
    heads = wh // hd
    n = t // BLK
    tall = pl.BlockSpec((t, BLK), lambda i: (0, i))
    return pl.pallas_call(
        functools.partial(forward_kernel, heads),
        grid=(n,),
        in_specs=[
            smem(), rows(d), whole(*gains.shape), whole(*wqkv.shape), whole(*wsel_t.shape),
            whole(*wout.shape),
        ],
        out_specs=[
            rows(d), rows(wh), rows(wh), rows(wh), rows(hd), rows(hd), tall,
            pl.BlockSpec((8, BLK), lambda i: (0, i)), rows(wh), rows(d),
        ],
        out_shape=[
            shape((t, d), BF), shape((t, wh), BF), shape((t, wh), BF), shape((t, wh), BF),
            shape((t, hd), BF), shape((t, hd), BF), shape((t, t), F32), shape((8, t), F32),
            shape((t, wh), BF), shape((t, d), BF),
        ],
        scratch_shapes=[
            pltpu.VMEM((t, wh), BF), pltpu.VMEM((wh, t), BF), pltpu.VMEM((t, hd), BF),
            pltpu.VMEM((t, 128), F32), pltpu.VMEM((heads // 2, 2 * hd, 2 * BLK), BF),
            pltpu.VMEM((t, 128), jnp.int32), pltpu.VMEM((8, 2 * BLK), F32),
            pltpu.VMEM((8, 2 * BLK), F32), pltpu.VMEM((wh, BLK), F32),
        ],
        compiler_params=params(),
        cost_estimate=cost(2 * t * d * (4 * wh + 2 * hd) + 4 * heads * t * t * hd, 16 * MIB, heads * t * t),
        name="attention_forward",
    )(lens, x, gains, wqkv, wsel_t, wout)


def feed_kernel(
    half, x, part_a, part_b, gains, up, down, g, mid_o, h2_o, act_o, du_o, dn_o, dsend_o,
    act_s,
):
    step = pl.program_id(0)
    here = rows_of(step)
    mid = x[...].astype(F32) + (part_a[...].astype(F32) + part_b[...].astype(F32))
    mid_o[...] = mid
    h2 = (mid * norm_scale(mid) * gains[1:2, :]).astype(BF)
    h2_o[...] = h2
    hidden = up.shape[1]
    chunk = hidden
    cuts = [slice(c, c + chunk) for c in range(0, hidden, chunk)]
    ups = [mm(h2, up[:, cut]) for cut in cuts]
    das = [mm_nt(g[here, :], down[cut, :]) for cut in cuts]
    dus = []
    for u, da, cut in zip(ups, das, cuts):
        u2 = u * u
        curve = jnp.tanh(u * (CURVE + (CURVE * CUBE) * u2))
        part = 0.5 * (1.0 + curve)
        act = (u * part).astype(BF)
        slope = part + (0.5 * u) * (1.0 - curve * curve) * (CURVE + (3.0 * CURVE * CUBE) * u2)
        du = (da * slope).astype(BF)
        act_o[:, cut] = act
        act_s[here, cut] = act
        du_o[:, cut] = du
        dus.append(du)
    dn = functools.reduce(jnp.add, [mm_nt(du, up[:, cut]) for du, cut in zip(dus, cuts)])
    dn_o[...] = dn.astype(BF)

    @pl.when(step == pl.num_programs(0) - 1)
    def _():
        size = dsend_o.shape[0]
        at = pl.ds(pl.multiple_of(half[0] * size, 128), size)
        dsend_o[...] = mm_tn(act_s[:, at], g[...]).astype(BF)


def feed(half, x, part_a, part_b, gains, up, down, g):
    t, d = x.shape
    hidden = up.shape[1]
    return pl.pallas_call(
        feed_kernel,
        grid=(t // BLK,),
        in_specs=[
            smem(), rows(d), rows(d), rows(d), whole(*gains.shape), whole(*up.shape),
            whole(*down.shape), whole(t, d),
        ],
        out_specs=[
            rows(d), rows(d), rows(hidden), rows(hidden), rows(d), whole(hidden // 2, d),
        ],
        out_shape=[
            shape((t, d), F32), shape((t, d), BF), shape((t, hidden), BF), shape((t, hidden), BF),
            shape((t, d), BF), shape((hidden // 2, d), BF),
        ],
        scratch_shapes=[pltpu.VMEM((t, hidden), BF)],
        compiler_params=params(),
        cost_estimate=cost(8 * t * d * hidden, 24 * MIB, t * hidden),
        name="feed_forward",
    )(half, x, part_a, part_b, gains, up, down, g)


def product_kernel(half, left, right, out):
    out[...] = mm_tn(left[...], right[...]).astype(BF)


def down_half(half, act, g):
    t, hidden = act.shape
    d = g.shape[1]
    tiles = 3
    tile = hidden // 2 // tiles
    return pl.pallas_call(
        product_kernel,
        grid_spec=pltpu.PrefetchScalarGridSpec(
            num_scalar_prefetch=1,
            grid=(tiles,),
            in_specs=[
                pl.BlockSpec((t, tile), lambda j, half: (0, half[0] * tiles + j)),
                whole(t, d),
            ],
            out_specs=pl.BlockSpec((tile, d), lambda j, half: (j, 0)),
        ),
        out_shape=shape((hidden // 2, d), BF),
        compiler_params=params(),
        cost_estimate=cost(t * d * hidden, 6 * MIB),
        name="grad_down",
    )(half, act, g)


def norm_back(values, scale, gain, grad):
    unit = values * scale
    grad_unit = grad * gain
    mean = jnp.mean(grad_unit * unit, axis=-1, keepdims=True)
    return scale * (grad_unit - unit * mean), jnp.sum(grad * unit, axis=0, keepdims=True)


def middle_kernel(
    hd, half, mid, part_a, part_b, gains, g, wout, mixed_row, mixed_in, h2_in, du_in, dmid_o,
    dmix_o, dots_o, send_o, keep_o, gain_o, gm_s, mixed, h2, du, sems,
):
    step = pl.program_id(0)
    here = rows_of(step)
    final = step == pl.num_programs(0) - 1
    late = [
        (source, target, sems.at[n])
        for n, (source, target) in enumerate(((h2_in, h2), (du_in, du), (mixed_in, mixed)))
    ]
    fetch(step == 0, None, *late)
    values = mid[...]
    grad = part_a[...].astype(F32) + part_b[...].astype(F32)
    back, gain_grad = norm_back(values, norm_scale(values), gains[1:2, :], grad)
    dmid = g[...].astype(F32) + back
    dmid_o[...] = dmid
    gm = dmid.astype(BF)
    gm_s[here, :] = gm
    dmix = mm_nt(gm, wout[...]).astype(BF)
    dmix_o[...] = dmix
    both = (dmix.astype(F32) * mixed_row[...].astype(F32)).T
    for h in range(both.shape[0] // hd):
        dots_o[h : h + 1, :] = jnp.sum(both[h * hd : (h + 1) * hd, :], axis=0, keepdims=True)

    @pl.when(step == 0)
    def _():
        gain_o[...] = jnp.zeros_like(gain_o)

    gain_o[0:1, :] += gain_grad
    fetch(None, final, *late)

    @pl.when(final)
    def _():
        hidden = du.shape[1]
        size = send_o.shape[0]
        for which, into in ((half[0], send_o), (1 - half[0], keep_o)):
            at = pl.ds(pl.multiple_of(which * size, 128), size)
            into[:, :hidden] = mm_tn(h2[:, at], du[...]).astype(BF)
            into[:, hidden:] = mm_tn(mixed[...], gm_s[:, at]).astype(BF)


def middle(half, mid, part_a, part_b, gains, g, wout, mixed, h2, du, hd):
    t, d = mid.shape
    wh = wout.shape[0]
    hidden = du.shape[1]
    return pl.pallas_call(
        functools.partial(middle_kernel, hd),
        grid=(t // BLK,),
        in_specs=[
            smem(), rows(d), rows(d), rows(d), whole(*gains.shape), rows(d), whole(*wout.shape),
            rows(wh), anywhere(), anywhere(), anywhere(),
        ],
        out_specs=[
            rows(d), rows(wh), pl.BlockSpec((8, BLK), lambda i: (0, i)),
            whole(d // 2, hidden + d // 2), whole(d // 2, hidden + d // 2), whole(8, d),
        ],
        out_shape=[
            shape((t, d), F32), shape((t, wh), BF), shape((8, t), F32),
            shape((d // 2, hidden + d // 2), BF), shape((d // 2, hidden + d // 2), BF),
            shape((8, d), F32),
        ],
        scratch_shapes=[
            pltpu.VMEM((t, d), BF), pltpu.VMEM((t, wh), BF), pltpu.VMEM((t, d), BF),
            pltpu.VMEM((t, hidden), BF), pltpu.SemaphoreType.DMA((3,)),
        ],
        compiler_params=params(),
        cost_estimate=cost(2 * t * d * wh + t * d * hidden, 20 * MIB),
        name="second_norm_backward",
    )(half, mid, part_a, part_b, gains, g, wout, mixed, mixed, h2, du)


def split_three(values):
    one = values.astype(BF).astype(F32)
    rest = values - one
    two = rest.astype(BF).astype(F32)
    return one, two, (rest - two).astype(BF).astype(F32)


def backward_kernel(
    n_blocks, heads, lens, half, q, k, v, sq, sk, pen, lse, dots, dmix, h1_in, cat_o, send_o, keep_o,
    qx_s, qm_s, dx_s, dm_s, dq_s, dsq_s, dk_s, dv_s, dsk_s, kt_s, skt_s, kx_s, vx_s, seg_s, h1, sems,
):
    j = pl.program_id(0)
    late = (h1_in, h1, sems.at[0])
    fetch(j == 0, None, late)
    wh = k.shape[1]
    hd = sk.shape[1]
    t = q.shape[0]
    two = 2 * hd
    pairs = heads // 2
    scale = hd**-0.5
    lane = lax.broadcasted_iota(jnp.int32, (1, two), 1)
    side_of = [lane // hd == side for side in range(2)]
    ones = jnp.broadcast_to(jnp.where(lane < 3, 1.0, 0.0).astype(BF), (BLK, two))

    @pl.when(j == 0)
    def _():
        dq_s[...] = jnp.zeros_like(dq_s)
        dsq_s[...] = jnp.zeros_like(dsq_s)
        seg, _ = sequence_ids(lens, lax.broadcasted_iota(jnp.int32, (1, t), 1))
        seg_s[0:1, :] = seg

        tall = lax.broadcasted_iota(jnp.int32, (two, 1), 0)

        def prepare(i, _):
            at = rows_of(i)
            for which, (source, plain, wide) in enumerate(((q, qm_s, qx_s), (dmix, dm_s, dx_s))):
                source_t = source[at, :].astype(F32).T
                for h in range(heads):
                    side = h % 2
                    pair = slice((h // 2) * two, (h // 2 + 1) * two)
                    cut = slice(side * BLK, (side + 1) * BLK)
                    value = jnp.where(side_of[side], source[at, pair], jnp.zeros((), BF))
                    plain[h // 2, i, cut, :] = value
                    value = jnp.where(tall // hd == side, source_t[pair, :], 0.0)
                    wide[h // 2, i, 0:two, cut] = value.astype(BF)
                    one, mid, low = split_three(-(lse, dots)[which][h : h + 1, at])
                    value = jnp.where(tall == 0, one, jnp.where(tall == 1, mid, jnp.where(tall == 2, low, 0.0)))
                    wide[h // 2, i, two : 2 * two, cut] = value.astype(BF)
            return 0

        lax.fori_loop(0, n_blocks, prepare, 0)

    here = rows_of(j)
    dk_s[...] = jnp.zeros_like(dk_s)
    dv_s[...] = jnp.zeros_like(dv_s)
    dsk_s[...] = jnp.zeros_like(dsk_s)
    kt_s[...] = k[...].astype(F32).T.astype(BF)
    skt_s[...] = sk[...].astype(F32).T.astype(BF)
    for p in range(pairs):
        pair = slice(p * two, (p + 1) * two)
        kx_s[p, :, 0:two] = k[:, pair]
        vx_s[p, :, 0:two] = v[:, pair]
        kx_s[p, :, two:] = ones
        vx_s[p, :, two:] = ones
    after = triangle(True)
    col = j * BLK + lax.broadcasted_iota(jnp.int32, (BLK, 1), 0)
    seg_j, first_j = sequence_ids(lens, col)
    seg_j = jnp.where(first_j, -1, seg_j)

    def tile(back, carry):
        i = n_blocks - 1 - back
        at = rows_of(i)
        bias = pen[:, at]
        bias = jnp.concatenate([bias, bias], axis=1)
        scores = [mm(kx_s[p], qx_s[p, i]) - bias for p in range(pairs)]
        dprobs = [mm(vx_s[p], dx_s[p, i]) for p in range(pairs)]
        sel = jnp.maximum(mm_nt(sk[...], sq[at, :]), 0.0)
        dpen = None
        probs, lows = [], []
        for p in range(pairs):
            prob = jnp.exp(scores[p])
            dscore = prob * dprobs[p]
            both = dscore[:, :BLK] + dscore[:, BLK:]
            dpen = both if dpen is None else dpen + both
            probs.append(prob.astype(BF))
            lows.append(dscore.astype(BF))
        for p in range(pairs):
            pair = slice(p * two, (p + 1) * two)
            for side in range(2):
                h = 2 * p + side
                dq_s[p, side * hd : (side + 1) * hd, at] += mm(
                    kt_s[h * hd : (h + 1) * hd, :], lows[p][:, side * BLK : (side + 1) * BLK]
                )
            dv_s[:, pair] += mm(probs[p], dm_s[p, i])
            dk_s[:, pair] += mm(lows[p], qm_s[p, i])
        dpicked = split_dot(dpen, after) + carry
        row = i * BLK + lax.broadcasted_iota(jnp.int32, (1, BLK), 1)
        chosen = (seg_j == seg_s[0:1, at]) & (col < row)
        dsel = jnp.where(chosen, -2.0 * dpicked * sel, 0.0).astype(BF)
        dsk_s[...] += mm(dsel, sq[at, :])
        dsq_s[:, at] += mm(skt_s[...], dsel)
        return dpicked[:, 0:1] + dpen[:, 0:1]

    lax.fori_loop(0, n_blocks - j, tile, jnp.zeros((BLK, 1), F32))
    cat_o[here, wh : 2 * wh] = dk_s[...].astype(BF)
    cat_o[here, 2 * wh : 3 * wh] = dv_s[...].astype(BF)
    cat_o[here, 3 * wh + hd : 3 * wh + 2 * hd] = dsk_s[...].astype(BF)

    fetch(None, j == n_blocks - 1, late)

    @pl.when(j == n_blocks - 1)
    def _():
        for p in range(pairs):
            cat_o[:, p * two : (p + 1) * two] = (dq_s[p] * scale).T.astype(BF)
        cat_o[:, 3 * wh : 3 * wh + hd] = (dsq_s[...] * scale).T.astype(BF)
        size = send_o.shape[0]
        for which, into in ((half[0], send_o), (1 - half[0], keep_o)):
            at = pl.ds(pl.multiple_of(which * size, 128), size)
            into[...] = mm_tn(h1[:, at], cat_o[...]).astype(BF)


def backward(lens, half, q, k, v, sq, sk, pen, lse, dots, dmix, h1):
    d = h1.shape[1]
    t, wh = q.shape
    hd = sq.shape[1]
    heads = wh // hd
    n = t // BLK
    width = 3 * wh + 2 * hd
    per_head = pltpu.VMEM((heads // 2, n, 2 * BLK, 2 * hd), BF)
    per_head_t = pltpu.VMEM((heads // 2, n, 4 * hd, 2 * BLK), BF)
    return pl.pallas_call(
        functools.partial(backward_kernel, n, heads),
        grid=(n,),
        in_specs=[
            smem(), smem(), whole(t, wh), rows(wh), rows(wh), whole(t, hd), rows(hd), rows(t),
            whole(8, t), whole(8, t), whole(t, wh), anywhere(),
        ],
        out_specs=[whole(t, width), whole(d // 2, width), whole(d // 2, width)],
        out_shape=[
            shape((t, width), BF), shape((d // 2, width), BF), shape((d // 2, width), BF),
        ],
        scratch_shapes=[
            per_head_t, per_head, per_head_t, per_head, pltpu.VMEM((heads // 2, 2 * hd, t), F32),
            pltpu.VMEM((hd, t), F32), pltpu.VMEM((BLK, wh), F32),
            pltpu.VMEM((BLK, wh), F32), pltpu.VMEM((BLK, hd), F32), pltpu.VMEM((wh, BLK), BF),
            pltpu.VMEM((hd, BLK), BF), pltpu.VMEM((heads // 2, BLK, 4 * hd), BF),
            pltpu.VMEM((heads // 2, BLK, 4 * hd), BF), pltpu.VMEM((8, t), jnp.int32),
            pltpu.VMEM((t, d), BF), pltpu.SemaphoreType.DMA((1,)),
        ],
        compiler_params=params(),
        cost_estimate=cost(10 * heads * t * t * hd, 12 * MIB, heads * t * t),
        name="attention_backward",
    )(lens, half, q, k, v, sq, sk, pen, lse, dots, dmix, h1)


def first_kernel(cat, wqkv, wsel, out):
    wh = wqkv.shape[2]
    total = mm(cat[:, 3 * wh :], wsel[...])
    for i in range(3):
        total = total + mm_nt(cat[:, i * wh : (i + 1) * wh], wqkv[i])
    out[...] = total.astype(BF)


def first_grad(cat, wqkv, wsel):
    t, width = cat.shape
    d = wqkv.shape[1]
    return pl.pallas_call(
        first_kernel,
        grid=(t // BLK,),
        in_specs=[rows(width), whole(*wqkv.shape), whole(*wsel.shape)],
        out_specs=rows(d),
        out_shape=shape((t, d), BF),
        compiler_params=params(),
        cost_estimate=cost(2 * t * d * width, 6 * MIB, share=SHARES[0]),
        name="first_norm_grad",
    )(cat, wqkv, wsel)


def finish_kernel(
    x, part_a, part_b, gains, dmid, mid, fold_a, fold_b, grad_o, out_o, gain_o
):
    values = x[...].astype(F32)
    grad = part_a[...].astype(F32) + part_b[...].astype(F32)
    back, gain_grad = norm_back(values, norm_scale(values), gains[0:1, :], grad)
    grad_o[...] = dmid[...] + back
    out_o[...] = (mid[...] + (fold_a[...].astype(F32) + fold_b[...].astype(F32))).astype(BF)

    @pl.when(pl.program_id(0) == 0)
    def _():
        gain_o[...] = jnp.zeros_like(gain_o)

    gain_o[0:1, :] += gain_grad


def finish(x, part_a, part_b, gains, dmid, mid, fold_a, fold_b):
    t, d = x.shape
    return pl.pallas_call(
        finish_kernel,
        grid=(t // BLK,),
        in_specs=[rows(d), rows(d), rows(d), whole(*gains.shape)] + [rows(d)] * 4,
        out_specs=[rows(d), rows(d), whole(8, d)],
        out_shape=[shape((t, d), F32), shape((t, d), BF), shape((8, d), F32)],
        compiler_params=params(),
        cost_estimate=cost(24 * t * d, 20 * MIB, share=SHARES[2]),
        name="first_norm_backward",
    )(x, part_a, part_b, gains, dmid, mid, fold_a, fold_b)


def branch_kernel(act, down, out):
    out[...] = mm(act[...], down[...]).astype(BF)


def branch(act, down):
    t, hidden = act.shape
    d = down.shape[1]
    return pl.pallas_call(
        branch_kernel,
        grid=(t // BLK,),
        in_specs=[rows(hidden), whole(*down.shape)],
        out_specs=rows(d),
        out_shape=shape((t, d), BF),
        compiler_params=params(),
        cost_estimate=cost(2 * t * d * hidden, 8 * MIB, share=SHARES[1]),
        name="down_projection",
    )(act, down)


class Sum:
    def __init__(self, n_dp, n_tensor, orders):
        self.n_dp, self.n_tensor = n_dp, n_tensor
        self.stages = n_dp.bit_length() - 1
        rest = list(range(4, self.stages))
        self.orders = [[1 << b for b in list(orders[t % 2]) + rest] for t in range(n_tensor)]
        self.dp = lax.axis_index("dp")
        self.tensor = lax.axis_index("tensor")

    def place(self, stage):
        out = (self.dp // self.orders[0][stage]) % 2
        for t in range(1, self.n_tensor):
            out = jnp.where(self.tensor == t, (self.dp // self.orders[t][stage]) % 2, out)
        return out

    def swap(self, value, stage):
        pairs = [
            (i * self.n_tensor + t, (i ^ self.orders[t][stage]) * self.n_tensor + t)
            for i in range(self.n_dp)
            for t in range(self.n_tensor)
        ]
        return lax.ppermute(value, ("dp", "tensor"), pairs)

    def split(self, stage, *terms):
        size = terms[0].shape[0] // 2
        place = self.place(stage)

        def cut(which):
            pieces = [lax.dynamic_slice_in_dim(v, which * size, size, 0) for v in terms]
            return (pieces[0].astype(F32) + pieces[1].astype(F32)).astype(BF)

        return [cut(1 - place), cut(place)]

    def join(self, stage, mine, other):
        place = self.place(stage)
        low, high = jnp.where(place == 0, mine, other), jnp.where(place == 0, other, mine)
        return jnp.concatenate([low, high], axis=0)


class Chain:
    def __init__(self, sums, line):
        self.sums, self.line, self.stage = sums, line, 0

    def begin(self, send):
        self.got = self.sums.swap(send, 0)

    def hold(self, keep):
        self.keep = keep

    def reduce(self):
        sums, self.stage = self.sums, self.stage + 1
        if self.stage < sums.stages:
            split = functools.partial(sums.split, self.stage)
            send, self.keep = self.line.run(split, self.keep, self.got)
            self.got = sums.swap(send, self.stage)
        else:
            add = lambda a, b: [(a.astype(F32) + b.astype(F32)).astype(BF)]
            (self.piece,) = self.line.run(add, self.keep, self.got)
            self.spread()

    def spread(self):
        self.stage -= 1
        self.got = self.sums.swap(self.piece, self.stage)

    def gather(self):
        join = lambda *v: [self.sums.join(self.stage, *v)]
        (self.piece,) = self.line.run(join, self.piece, self.got)
        self.spread()

    def step(self):
        if not hasattr(self, "piece"):
            self.reduce()
        elif self.stage > 0:
            self.gather()
        else:
            return False
        return True

    def halves(self):
        return self.piece, self.got


class Line:
    def __init__(self):
        self.token = None

    def run(self, step, *values, after=()):
        if self.token is not None:
            first, *_ = lax.optimization_barrier((values[0], self.token, *after))
            values = (first, *values[1:])
        out = step(*values)
        self.token = out[0]
        return out


def swap_tensor(value, n_tensor):
    return lax.ppermute(value, "tensor", [(t, t ^ 1) for t in range(n_tensor)])


def join_kernel(side, mine, other, out):
    @pl.when(pl.program_id(0) == 0)
    def _():
        out[...] = mine[...].astype(F32)

    @pl.when(pl.program_id(0) == 1)
    def _():
        out[...] = other[...].astype(F32)


def join(side, mine, other):
    r, n = mine.shape
    tiles = 3
    tile = r // tiles
    return pl.pallas_call(
        join_kernel,
        grid_spec=pltpu.PrefetchScalarGridSpec(
            num_scalar_prefetch=1,
            grid=(2, tiles),
            in_specs=[
                pl.BlockSpec((tile, n), lambda s, j, side: (jnp.where(s == 0, j, tiles - 1), 0)),
                pl.BlockSpec((tile, n), lambda s, j, side: (jnp.where(s == 0, 0, j), 0)),
            ],
            out_specs=pl.BlockSpec(
                (tile, n), lambda s, j, side: (jnp.where(s == 0, side[0], 1 - side[0]) * tiles + j, 0)
            ),
        ),
        out_shape=shape((2 * r, n), F32),
        compiler_params=pltpu.CompilerParams(
            dimension_semantics=("arbitrary", "arbitrary"), vmem_limit_bytes=32 * MIB
        ),
        cost_estimate=cost(0, 12 * r * n, share=SHARES[3]),
        name="join_halves",
    )(side, mine, other)


def join_up_kernel(side, mine, other, up_o, out_o):
    def put(piece):
        up_o[...] = piece[:, : up_o.shape[1]].astype(F32)
        out_o[...] = piece[:, up_o.shape[1] :].astype(F32)

    pl.when(pl.program_id(0) == 0)(lambda: put(mine[...]))
    pl.when(pl.program_id(0) == 1)(lambda: put(other[...]))


def join_up(side, mine, other, hidden, wh):
    r, n = mine.shape
    place = lambda s, side: jnp.where(s == 0, side[0], 1 - side[0])
    return pl.pallas_call(
        join_up_kernel,
        grid_spec=pltpu.PrefetchScalarGridSpec(
            num_scalar_prefetch=1,
            grid=(2,),
            in_specs=[pl.BlockSpec((r, n), lambda s, side: (0, 0))] * 2,
            out_specs=[
                pl.BlockSpec((r, hidden), lambda s, side: (place(s, side), 0)),
                pl.BlockSpec((wh, r), lambda s, side: (0, place(s, side))),
            ],
        ),
        out_shape=[shape((2 * r, hidden), F32), shape((wh, 2 * r), F32)],
        compiler_params=params(32),
        cost_estimate=cost(0, 12 * r * n, share=SHARES[4]),
        name="join_up",
    )(side, mine, other)


def join_attention_kernel(wh, side, mine, other, qkv_o, sel_o):
    def put(piece):
        for i in range(3):
            qkv_o[i] = piece[:, i * wh : (i + 1) * wh].astype(F32)
        sel_o[...] = piece[:, 3 * wh :].astype(F32)

    pl.when(pl.program_id(0) == 0)(lambda: put(mine[...]))
    pl.when(pl.program_id(0) == 1)(lambda: put(other[...]))


def join_attention(side, mine, other, wh, hd):
    r, n = mine.shape
    place = lambda s, side: jnp.where(s == 0, side[0], 1 - side[0])
    return pl.pallas_call(
        functools.partial(join_attention_kernel, wh),
        grid_spec=pltpu.PrefetchScalarGridSpec(
            num_scalar_prefetch=1,
            grid=(2,),
            in_specs=[pl.BlockSpec((r, n), lambda s, side: (0, 0))] * 2,
            out_specs=[
                pl.BlockSpec((3, r, wh), lambda s, side: (0, place(s, side), 0)),
                pl.BlockSpec((r, 2 * hd), lambda s, side: (place(s, side), 0)),
            ],
        ),
        out_shape=[shape((3, 2 * r, wh), F32), shape((2 * r, 2 * hd), F32)],
        compiler_params=params(32),
        cost_estimate=cost(0, 12 * r * n, share=SHARES[5]),
        name="join_attention",
    )(side, mine, other)


def per_device(
    n_dp, n_tensor, inputs, seq_lengths, qkv_weight, out_weight, up_weight, down_weight,
    select_weight, norm_gains, grad_output,
):
    wh = qkv_weight.shape[2]
    hd = select_weight.shape[2]
    d = inputs.shape[1]
    hidden = up_weight.shape[1]
    line = Line()
    run = line.run
    sums = [Sum(n_dp, n_tensor, orders) for orders in (DOWN, UP, ATT)]
    down, up, att = (Chain(each, line) for each in sums)
    small = sums[0]
    down_kept, up_kept, att_kept = (
        each.place(0).reshape(1).astype(jnp.int32) for each in sums
    )
    select_t = jnp.swapaxes(select_weight, 1, 2)
    swap = functools.partial(swap_tensor, n_tensor=n_tensor)

    h1, q, k, v, sq, sk, pen, lse, mixed, part = run(
        forward, seq_lengths, inputs, norm_gains, qkv_weight, select_t, out_weight
    )
    mid, h2, act, du, dn2, down_send = run(
        lambda part, *v: feed(1 - down_kept, inputs, part, *v),
        part, swap(part), norm_gains, up_weight, down_weight, grad_output,
    )
    dn2_other = swap(dn2)
    down.begin(down_send)
    down.hold(*run(lambda act, *v: [down_half(down_kept, act, *v)], act, grad_output))
    dmid, dmix, dots, up_send, up_keep, gain_two = run(
        lambda dn2, *v: middle(1 - up_kept, mid, dn2, *v, hd),
        dn2, dn2_other, norm_gains, grad_output, out_weight, mixed, h2, du,
    )
    up.begin(up_send)
    up.hold(up_keep)
    steps = {"d": down.step, "u": up.step, "a": att.step}
    for letter in EARLY:
        steps[letter]()
    cat, att_send, att_keep = run(
        lambda dots, *v: backward(seq_lengths, 1 - att_kept, *v[:7], dots, *v[7:]),
        dots, q, k, v, sq, sk, pen, lse, dmix, h1,
    )
    att.begin(att_send)
    att.hold(att_keep)
    done = {}

    def first():
        value = (first_grad if FREE else over(first_grad))(cat, qkv_weight, select_t.reshape(2 * hd, d))
        done["dn1"] = value, swap(value)

    def fold():
        value = (branch if FREE else over(branch))(act, down_weight)
        done["fold"] = value, swap(value)

    def over(kernel):
        return lambda *v: run(lambda *w: [kernel(*w)], *v)[0]

    def last():
        done["inputs"], done["output"], gain_one = run(
            lambda dn1, *v: finish(inputs, dn1, *v),
            *done["dn1"], norm_gains, dmid, mid, *done["fold"],
        )
        done["gains"] = jnp.concatenate([gain_one[0:1], gain_two[0:1]], axis=0), 0

    def gain():
        value, stage = done["gains"]
        if stage == small.stages:
            return False
        (value,) = run(lambda *v: [v[0] + v[1]], value, small.swap(value, stage))
        done["gains"] = value, stage + 1
        return True

    def down_out():
        while down.step():
            pass
        (done["down"],) = run(lambda *v: [join(down_kept, *v)], *down.halves())

    def up_out():
        while up.step():
            pass
        done["up"] = run(lambda *v: join_up(up_kept, *v, hidden, wh), *up.halves())

    def att_out():
        while att.step():
            pass
        done["att"] = run(lambda *v: join_attention(att_kept, *v, wh, hd), *att.halves())

    steps.update(n=first, b=fold, f=last, g=gain, D=down_out, U=up_out, A=att_out)
    for letter in LATE:
        steps[letter]()
    while gain():
        pass
    grad_inputs, output, gains, grad_down = (done[k] for k in ("inputs", "output", "gains", "down"))
    gains = gains[0]
    grad_up, grad_out = done["up"]
    grad_qkv, select_part = done["att"]
    select_t_sum = select_part.T
    select_t_sum = select_t_sum + swap(select_t_sum)
    grad_select = jnp.swapaxes(select_t_sum.reshape(2, hd, d), 1, 2)
    return (output, grad_inputs, grad_qkv, grad_out, grad_up, grad_down, grad_select, gains)


def solution(mesh):
    placed = (
        P("dp", None),
        P("dp", None),
        P(None, None, "tensor"),
        P("tensor", None),
        P(None, "tensor"),
        P("tensor", None),
        P(),
        P(),
        P("dp", None),
    )
    return jax.shard_map(
        functools.partial(per_device, mesh.shape["dp"], mesh.shape["tensor"]),
        mesh=mesh,
        in_specs=placed,
        out_specs=(
            P("dp", None),
            P("dp", None),
            P(None, None, "tensor"),
            P("tensor", None),
            P(None, "tensor"),
            P("tensor", None),
            P(),
            P(),
        ),
        check_vma=False,
    )
```

```python
import functools

import jax
import jax.numpy as jnp
from jax import lax
from jax.experimental import pallas as pl
from jax.experimental.pallas import tpu as pltpu
from jax.sharding import PartitionSpec as P

BF = jnp.bfloat16
F32 = jnp.float32
EPS = 1e-6
BLK = 256
NOT_ATTENDED = 1e30
CURVE = 0.7978845608028654
CUBE = 0.044715
MIB = 1024 * 1024
COST = 1.0

DOWN = (0, 1, 2, 3), (1, 2, 0, 3)
UP = (2, 0, 1, 3), (1, 2, 0, 3)
ATT = (0, 1, 2, 3), (2, 0, 1, 3)
EARLY = "d"
LATE = "dbudnudaufuadaudaugadugaagDgAU"
FREE = False

SHARES = (3.0, 3.0, 3.0, 3.0, 3.0, 3.0)


def mm(a, b):
    return jnp.dot(a, b, preferred_element_type=F32)


def mm_nt(a, b):
    return lax.dot_general(a, b, (((1,), (1,)), ((), ())), preferred_element_type=F32)


def mm_tn(a, b):
    return lax.dot_general(a, b, (((0,), (0,)), ((), ())), preferred_element_type=F32)


def params(limit_mib=56):
    return pltpu.CompilerParams(
        dimension_semantics=("arbitrary",), vmem_limit_bytes=limit_mib * MIB
    )


def cost(flops, nbytes, trans=0, share=1.0):
    return pl.CostEstimate(
        flops=int(COST * share * flops), bytes_accessed=int(COST * share * nbytes),
        transcendentals=int(COST * share * trans),
    )


def shape(dims, dtype):
    return jax.ShapeDtypeStruct(tuple(dims), dtype)


def whole(*dims):
    return pl.BlockSpec(tuple(dims), lambda *_: (0,) * len(dims))


def rows(width, count=BLK):
    return pl.BlockSpec((count, width), lambda i, *_: (i, 0))


def anywhere():
    return pl.BlockSpec(memory_space=pl.ANY)


def fetch(start, wait, *copies):
    for condition, act in ((start, "start"), (wait, "wait")):
        if condition is None:
            continue

        @pl.when(condition)
        def _():
            for copy in copies:
                getattr(pltpu.make_async_copy(*copy), act)()


def smem():
    return pl.BlockSpec(memory_space=pltpu.SMEM)


def sequence_ids(lens, pos):
    seg = jnp.zeros(pos.shape, jnp.int32)
    first = jnp.zeros(pos.shape, jnp.bool_)
    end = jnp.int32(0)
    for s in range(lens.shape[1]):
        length = lens[0, s]
        first = first | ((pos == end) & (length > 0))
        end = end + length
        seg = seg + (pos >= end).astype(jnp.int32)
    seg = jnp.where(pos < end, seg, lens.shape[1] + 1 + pos)
    return seg, first


def split_dot(values, ones):
    high = values.astype(BF)
    low = (values - high.astype(F32)).astype(BF)
    return mm(high, ones) + mm(low, ones)


def norm_scale(values):
    return lax.rsqrt(jnp.mean(values * values, axis=-1, keepdims=True) + EPS)


def rows_of(i):
    return pl.ds(pl.multiple_of(i * BLK, BLK), BLK)


def triangle(later):
    first = lax.broadcasted_iota(jnp.int32, (BLK, BLK), 0)
    second = lax.broadcasted_iota(jnp.int32, (BLK, BLK), 1)
    return jnp.where(first > second if later else first < second, 1.0, 0.0).astype(BF)


def forward_kernel(
    heads, lens, x, gains, wqkv, wsel_t, wout,
    h1_o, q_o, k_o, v_o, sq_o, sk_o, pen_o, lse_o, mix_o, part_o,
    k_s, vt_s, sk_s, carry_s, qx_s, seg_s, top_s, sum_s, acc_s,
):
    step = pl.program_id(0)
    hd = wsel_t.shape[1]
    t = k_s.shape[0]
    two = 2 * hd
    pairs = heads // 2
    scale = hd**-0.5
    here = rows_of(step)

    @pl.when(step == 0)
    def _():
        carry_s[...] = jnp.zeros_like(carry_s)
        qx_s[...] = jnp.zeros_like(qx_s)
        seg, first = sequence_ids(lens, lax.broadcasted_iota(jnp.int32, (t, 1), 0))
        seg_s[:, 0:1] = seg
        seg_s[:, 1:2] = jnp.where(first, -1, seg)

    xf = x[...].astype(F32)
    h1 = (xf * norm_scale(xf) * gains[0:1, :]).astype(BF)
    h1_o[...] = h1
    q32, k32, v32 = (mm(h1, wqkv[i]) for i in range(3))
    sq32, sk32 = (mm_nt(h1, wsel_t[i]) for i in range(2))
    q = (q32.astype(BF) * scale).astype(BF)
    q_t = (q32.T.astype(BF) * scale).astype(BF)
    k = k32.astype(BF)
    sq = (sq32.astype(BF) * scale).astype(BF)
    sk = sk32.astype(BF)
    q_o[...] = q
    k_o[...] = k
    v_o[...] = v32.astype(BF)
    sq_o[...] = sq
    sk_o[...] = sk
    k_s[here, :] = k
    sk_s[here, :] = sk
    vt_s[:, here] = v32.T.astype(BF)
    for p in range(pairs):
        for side in range(2):
            h = 2 * p + side
            qx_s[p, side * hd : (side + 1) * hd, side * BLK : (side + 1) * BLK] = q_t[
                h * hd : (h + 1) * hd, :
            ]

    row = step * BLK + lax.broadcasted_iota(jnp.int32, (1, BLK), 1)
    seg_i, _ = sequence_ids(lens, row)
    before = triangle(False)
    top_s[...] = jnp.full_like(top_s, -NOT_ATTENDED)
    sum_s[...] = jnp.zeros_like(sum_s)
    acc_s[...] = jnp.zeros_like(acc_s)

    def tile(j, _):
        at = rows_of(j)
        raw = [mm(k_s[at, p * two : (p + 1) * two], qx_s[p]) for p in range(pairs)]
        col = j * BLK + lax.broadcasted_iota(jnp.int32, (BLK, 1), 0)
        sel = jnp.maximum(mm_nt(sk_s[at, :], sq), 0.0)
        picked = jnp.where((seg_s[at, 1:2] == seg_i) & (col < row), sel * sel, 0.0)
        pen = split_dot(picked, before) + carry_s[at, 0:1]
        carry_s[at, 0:1] = pen[:, BLK - 1 : BLK] + picked[:, BLK - 1 : BLK]
        bias = jnp.where((seg_s[at, 0:1] == seg_i) & (col <= row), pen, NOT_ATTENDED)
        pen_o[at, :] = bias
        bias = jnp.concatenate([bias, bias], axis=1)
        lows, fades = [], []
        for p in range(pairs):
            s = raw[p] - bias
            old = top_s[p : p + 1, :]
            top = jnp.maximum(old, jnp.max(s, axis=0, keepdims=True))
            fade = jnp.exp(old - top)
            prob = jnp.exp(s - top)
            top_s[p : p + 1, :] = top
            sum_s[p : p + 1, :] = sum_s[p : p + 1, :] * fade + jnp.sum(prob, axis=0, keepdims=True)
            lows.append(prob.astype(BF))
            fades.append(fade)
        for h in range(heads):
            p, cut = h // 2, slice((h % 2) * BLK, (h % 2 + 1) * BLK)
            mine = slice(h * hd, (h + 1) * hd)
            acc_s[mine, :] = acc_s[mine, :] * fades[p][:, cut] + mm(vt_s[mine, at], lows[p][:, cut])
        return 0

    lax.fori_loop(0, step + 1, tile, 0)
    for h in range(heads):
        p, cut = h // 2, slice((h % 2) * BLK, (h % 2 + 1) * BLK)
        total = sum_s[p : p + 1, cut]
        lse_o[h : h + 1, :] = top_s[p : p + 1, cut] + jnp.log(total)
        acc_s[h * hd : (h + 1) * hd, :] = acc_s[h * hd : (h + 1) * hd, :] / total
    mixed = acc_s[...].T.astype(BF)
    mix_o[...] = mixed
    part_o[...] = mm(mixed, wout[...]).astype(BF)


def forward(lens, x, gains, wqkv, wsel_t, wout):
    t, d = x.shape
    wh = wqkv.shape[2]
    hd = wsel_t.shape[1]
    heads = wh // hd
    n = t // BLK
    tall = pl.BlockSpec((t, BLK), lambda i: (0, i))
    return pl.pallas_call(
        functools.partial(forward_kernel, heads),
        grid=(n,),
        in_specs=[
            smem(), rows(d), whole(*gains.shape), whole(*wqkv.shape), whole(*wsel_t.shape),
            whole(*wout.shape),
        ],
        out_specs=[
            rows(d), rows(wh), rows(wh), rows(wh), rows(hd), rows(hd), tall,
            pl.BlockSpec((8, BLK), lambda i: (0, i)), rows(wh), rows(d),
        ],
        out_shape=[
            shape((t, d), BF), shape((t, wh), BF), shape((t, wh), BF), shape((t, wh), BF),
            shape((t, hd), BF), shape((t, hd), BF), shape((t, t), F32), shape((8, t), F32),
            shape((t, wh), BF), shape((t, d), BF),
        ],
        scratch_shapes=[
            pltpu.VMEM((t, wh), BF), pltpu.VMEM((wh, t), BF), pltpu.VMEM((t, hd), BF),
            pltpu.VMEM((t, 128), F32), pltpu.VMEM((heads // 2, 2 * hd, 2 * BLK), BF),
            pltpu.VMEM((t, 128), jnp.int32), pltpu.VMEM((8, 2 * BLK), F32),
            pltpu.VMEM((8, 2 * BLK), F32), pltpu.VMEM((wh, BLK), F32),
        ],
        compiler_params=params(),
        cost_estimate=cost(2 * t * d * (4 * wh + 2 * hd) + 4 * heads * t * t * hd, 16 * MIB, heads * t * t),
        name="attention_forward",
    )(lens, x, gains, wqkv, wsel_t, wout)


def feed_kernel(
    half, x, part_a, part_b, gains, up, down, g, mid_o, h2_o, act_o, du_o, dn_o, dsend_o,
    act_s,
):
    step = pl.program_id(0)
    here = rows_of(step)
    mid = x[...].astype(F32) + (part_a[...].astype(F32) + part_b[...].astype(F32))
    mid_o[...] = mid
    h2 = (mid * norm_scale(mid) * gains[1:2, :]).astype(BF)
    h2_o[...] = h2
    hidden = up.shape[1]
    chunk = hidden
    cuts = [slice(c, c + chunk) for c in range(0, hidden, chunk)]
    ups = [mm(h2, up[:, cut]) for cut in cuts]
    das = [mm_nt(g[here, :], down[cut, :]) for cut in cuts]
    dus = []
    for u, da, cut in zip(ups, das, cuts):
        u2 = u * u
        curve = jnp.tanh(u * (CURVE + (CURVE * CUBE) * u2))
        part = 0.5 * (1.0 + curve)
        act = (u * part).astype(BF)
        slope = part + (0.5 * u) * (1.0 - curve * curve) * (CURVE + (3.0 * CURVE * CUBE) * u2)
        du = (da * slope).astype(BF)
        act_o[:, cut] = act
        act_s[here, cut] = act
        du_o[:, cut] = du
        dus.append(du)
    dn = functools.reduce(jnp.add, [mm_nt(du, up[:, cut]) for du, cut in zip(dus, cuts)])
    dn_o[...] = dn.astype(BF)

    @pl.when(step == pl.num_programs(0) - 1)
    def _():
        size = dsend_o.shape[0]
        at = pl.ds(pl.multiple_of(half[0] * size, 128), size)
        dsend_o[...] = mm_tn(act_s[:, at], g[...]).astype(BF)


def feed(half, x, part_a, part_b, gains, up, down, g):
    t, d = x.shape
    hidden = up.shape[1]
    return pl.pallas_call(
        feed_kernel,
        grid=(t // BLK,),
        in_specs=[
            smem(), rows(d), rows(d), rows(d), whole(*gains.shape), whole(*up.shape),
            whole(*down.shape), whole(t, d),
        ],
        out_specs=[
            rows(d), rows(d), rows(hidden), rows(hidden), rows(d), whole(hidden // 2, d),
        ],
        out_shape=[
            shape((t, d), F32), shape((t, d), BF), shape((t, hidden), BF), shape((t, hidden), BF),
            shape((t, d), BF), shape((hidden // 2, d), BF),
        ],
        scratch_shapes=[pltpu.VMEM((t, hidden), BF)],
        compiler_params=params(),
        cost_estimate=cost(8 * t * d * hidden, 24 * MIB, t * hidden),
        name="feed_forward",
    )(half, x, part_a, part_b, gains, up, down, g)


def product_kernel(half, left, right, out):
    out[...] = mm_tn(left[...], right[...]).astype(BF)


def down_half(half, act, g):
    t, hidden = act.shape
    d = g.shape[1]
    tiles = 3
    tile = hidden // 2 // tiles
    return pl.pallas_call(
        product_kernel,
        grid_spec=pltpu.PrefetchScalarGridSpec(
            num_scalar_prefetch=1,
            grid=(tiles,),
            in_specs=[
                pl.BlockSpec((t, tile), lambda j, half: (0, half[0] * tiles + j)),
                whole(t, d),
            ],
            out_specs=pl.BlockSpec((tile, d), lambda j, half: (j, 0)),
        ),
        out_shape=shape((hidden // 2, d), BF),
        compiler_params=params(),
        cost_estimate=cost(t * d * hidden, 6 * MIB),
        name="grad_down",
    )(half, act, g)


def norm_back(values, scale, gain, grad):
    unit = values * scale
    grad_unit = grad * gain
    mean = jnp.mean(grad_unit * unit, axis=-1, keepdims=True)
    return scale * (grad_unit - unit * mean), jnp.sum(grad * unit, axis=0, keepdims=True)


def middle_kernel(
    hd, half, mid, part_a, part_b, gains, g, wout, mixed_row, mixed_in, h2_in, du_in, dmid_o,
    dmix_o, dots_o, send_o, keep_o, gain_o, gm_s, mixed, h2, du, sems,
):
    step = pl.program_id(0)
    here = rows_of(step)
    final = step == pl.num_programs(0) - 1
    late = [
        (source, target, sems.at[n])
        for n, (source, target) in enumerate(((h2_in, h2), (du_in, du), (mixed_in, mixed)))
    ]
    fetch(step == 0, None, *late)
    values = mid[...]
    grad = part_a[...].astype(F32) + part_b[...].astype(F32)
    back, gain_grad = norm_back(values, norm_scale(values), gains[1:2, :], grad)
    dmid = g[...].astype(F32) + back
    dmid_o[...] = dmid
    gm = dmid.astype(BF)
    gm_s[here, :] = gm
    dmix = mm_nt(gm, wout[...]).astype(BF)
    dmix_o[...] = dmix
    both = (dmix.astype(F32) * mixed_row[...].astype(F32)).T
    for h in range(both.shape[0] // hd):
        dots_o[h : h + 1, :] = jnp.sum(both[h * hd : (h + 1) * hd, :], axis=0, keepdims=True)

    @pl.when(step == 0)
    def _():
        gain_o[...] = jnp.zeros_like(gain_o)

    gain_o[0:1, :] += gain_grad
    fetch(None, final, *late)

    @pl.when(final)
    def _():
        hidden = du.shape[1]
        size = send_o.shape[0]
        for which, into in ((half[0], send_o), (1 - half[0], keep_o)):
            at = pl.ds(pl.multiple_of(which * size, 128), size)
            into[:, :hidden] = mm_tn(h2[:, at], du[...]).astype(BF)
            into[:, hidden:] = mm_tn(mixed[...], gm_s[:, at]).astype(BF)


def middle(half, mid, part_a, part_b, gains, g, wout, mixed, h2, du, hd):
    t, d = mid.shape
    wh = wout.shape[0]
    hidden = du.shape[1]
    return pl.pallas_call(
        functools.partial(middle_kernel, hd),
        grid=(t // BLK,),
        in_specs=[
            smem(), rows(d), rows(d), rows(d), whole(*gains.shape), rows(d), whole(*wout.shape),
            rows(wh), anywhere(), anywhere(), anywhere(),
        ],
        out_specs=[
            rows(d), rows(wh), pl.BlockSpec((8, BLK), lambda i: (0, i)),
            whole(d // 2, hidden + d // 2), whole(d // 2, hidden + d // 2), whole(8, d),
        ],
        out_shape=[
            shape((t, d), F32), shape((t, wh), BF), shape((8, t), F32),
            shape((d // 2, hidden + d // 2), BF), shape((d // 2, hidden + d // 2), BF),
            shape((8, d), F32),
        ],
        scratch_shapes=[
            pltpu.VMEM((t, d), BF), pltpu.VMEM((t, wh), BF), pltpu.VMEM((t, d), BF),
            pltpu.VMEM((t, hidden), BF), pltpu.SemaphoreType.DMA((3,)),
        ],
        compiler_params=params(),
        cost_estimate=cost(2 * t * d * wh + t * d * hidden, 20 * MIB),
        name="second_norm_backward",
    )(half, mid, part_a, part_b, gains, g, wout, mixed, mixed, h2, du)


def split_three(values):
    one = values.astype(BF).astype(F32)
    rest = values - one
    two = rest.astype(BF).astype(F32)
    return one, two, (rest - two).astype(BF).astype(F32)


def backward_kernel(
    n_blocks, heads, lens, half, q, k, v, sq, sk, pen, lse, dots, dmix, h1_in, cat_o, send_o, keep_o,
    qx_s, qm_s, dx_s, dm_s, dq_s, dsq_s, dk_s, dv_s, dsk_s, kt_s, skt_s, kx_s, vx_s, seg_s, h1, sems,
):
    j = pl.program_id(0)
    late = (h1_in, h1, sems.at[0])
    fetch(j == 0, None, late)
    wh = k.shape[1]
    hd = sk.shape[1]
    t = q.shape[0]
    two = 2 * hd
    pairs = heads // 2
    scale = hd**-0.5
    lane = lax.broadcasted_iota(jnp.int32, (1, two), 1)
    side_of = [lane // hd == side for side in range(2)]
    ones = jnp.broadcast_to(jnp.where(lane < 3, 1.0, 0.0).astype(BF), (BLK, two))

    @pl.when(j == 0)
    def _():
        dq_s[...] = jnp.zeros_like(dq_s)
        dsq_s[...] = jnp.zeros_like(dsq_s)
        seg, _ = sequence_ids(lens, lax.broadcasted_iota(jnp.int32, (1, t), 1))
        seg_s[0:1, :] = seg

        tall = lax.broadcasted_iota(jnp.int32, (two, 1), 0)

        def prepare(i, _):
            at = rows_of(i)
            for which, (source, plain, wide) in enumerate(((q, qm_s, qx_s), (dmix, dm_s, dx_s))):
                source_t = source[at, :].astype(F32).T
                for h in range(heads):
                    side = h % 2
                    pair = slice((h // 2) * two, (h // 2 + 1) * two)
                    cut = slice(side * BLK, (side + 1) * BLK)
                    value = jnp.where(side_of[side], source[at, pair], jnp.zeros((), BF))
                    plain[h // 2, i, cut, :] = value
                    value = jnp.where(tall // hd == side, source_t[pair, :], 0.0)
                    wide[h // 2, i, 0:two, cut] = value.astype(BF)
                    one, mid, low = split_three(-(lse, dots)[which][h : h + 1, at])
                    value = jnp.where(tall == 0, one, jnp.where(tall == 1, mid, jnp.where(tall == 2, low, 0.0)))
                    wide[h // 2, i, two : 2 * two, cut] = value.astype(BF)
            return 0

        lax.fori_loop(0, n_blocks, prepare, 0)

    here = rows_of(j)
    dk_s[...] = jnp.zeros_like(dk_s)
    dv_s[...] = jnp.zeros_like(dv_s)
    dsk_s[...] = jnp.zeros_like(dsk_s)
    kt_s[...] = k[...].astype(F32).T.astype(BF)
    skt_s[...] = sk[...].astype(F32).T.astype(BF)
    for p in range(pairs):
        pair = slice(p * two, (p + 1) * two)
        kx_s[p, :, 0:two] = k[:, pair]
        vx_s[p, :, 0:two] = v[:, pair]
        kx_s[p, :, two:] = ones
        vx_s[p, :, two:] = ones
    after = triangle(True)
    col = j * BLK + lax.broadcasted_iota(jnp.int32, (BLK, 1), 0)
    seg_j, first_j = sequence_ids(lens, col)
    seg_j = jnp.where(first_j, -1, seg_j)

    def tile(back, carry):
        i = n_blocks - 1 - back
        at = rows_of(i)
        bias = pen[:, at]
        bias = jnp.concatenate([bias, bias], axis=1)
        scores = [mm(kx_s[p], qx_s[p, i]) - bias for p in range(pairs)]
        dprobs = [mm(vx_s[p], dx_s[p, i]) for p in range(pairs)]
        sel = jnp.maximum(mm_nt(sk[...], sq[at, :]), 0.0)
        dpen = None
        probs, lows = [], []
        for p in range(pairs):
            prob = jnp.exp(scores[p])
            dscore = prob * dprobs[p]
            both = dscore[:, :BLK] + dscore[:, BLK:]
            dpen = both if dpen is None else dpen + both
            probs.append(prob.astype(BF))
            lows.append(dscore.astype(BF))
        dpicked = split_dot(dpen, after) + carry
        for p in range(pairs):
            pair = slice(p * two, (p + 1) * two)
            for side in range(2):
                h = 2 * p + side
                dq_s[p, side * hd : (side + 1) * hd, at] += mm(
                    kt_s[h * hd : (h + 1) * hd, :], lows[p][:, side * BLK : (side + 1) * BLK]
                )
            dv_s[:, pair] += mm(probs[p], dm_s[p, i])
            dk_s[:, pair] += mm(lows[p], qm_s[p, i])
        row = i * BLK + lax.broadcasted_iota(jnp.int32, (1, BLK), 1)
        chosen = (seg_j == seg_s[0:1, at]) & (col < row)
        dsel = jnp.where(chosen, -2.0 * dpicked * sel, 0.0).astype(BF)
        dsk_s[...] += mm(dsel, sq[at, :])
        dsq_s[:, at] += mm(skt_s[...], dsel)
        return dpicked[:, 0:1] + dpen[:, 0:1]

    lax.fori_loop(0, n_blocks - j, tile, jnp.zeros((BLK, 1), F32))
    cat_o[here, wh : 2 * wh] = dk_s[...].astype(BF)
    cat_o[here, 2 * wh : 3 * wh] = dv_s[...].astype(BF)
    cat_o[here, 3 * wh + hd : 3 * wh + 2 * hd] = dsk_s[...].astype(BF)

    fetch(None, j == n_blocks - 1, late)

    @pl.when(j == n_blocks - 1)
    def _():
        for p in range(pairs):
            cat_o[:, p * two : (p + 1) * two] = (dq_s[p] * scale).T.astype(BF)
        cat_o[:, 3 * wh : 3 * wh + hd] = (dsq_s[...] * scale).T.astype(BF)
        size = send_o.shape[0]
        for which, into in ((half[0], send_o), (1 - half[0], keep_o)):
            at = pl.ds(pl.multiple_of(which * size, 128), size)
            into[...] = mm_tn(h1[:, at], cat_o[...]).astype(BF)


def backward(lens, half, q, k, v, sq, sk, pen, lse, dots, dmix, h1):
    d = h1.shape[1]
    t, wh = q.shape
    hd = sq.shape[1]
    heads = wh // hd
    n = t // BLK
    width = 3 * wh + 2 * hd
    per_head = pltpu.VMEM((heads // 2, n, 2 * BLK, 2 * hd), BF)
    per_head_t = pltpu.VMEM((heads // 2, n, 4 * hd, 2 * BLK), BF)
    return pl.pallas_call(
        functools.partial(backward_kernel, n, heads),
        grid=(n,),
        in_specs=[
            smem(), smem(), whole(t, wh), rows(wh), rows(wh), whole(t, hd), rows(hd), rows(t),
            whole(8, t), whole(8, t), whole(t, wh), anywhere(),
        ],
        out_specs=[whole(t, width), whole(d // 2, width), whole(d // 2, width)],
        out_shape=[
            shape((t, width), BF), shape((d // 2, width), BF), shape((d // 2, width), BF),
        ],
        scratch_shapes=[
            per_head_t, per_head, per_head_t, per_head, pltpu.VMEM((heads // 2, 2 * hd, t), F32),
            pltpu.VMEM((hd, t), F32), pltpu.VMEM((BLK, wh), F32),
            pltpu.VMEM((BLK, wh), F32), pltpu.VMEM((BLK, hd), F32), pltpu.VMEM((wh, BLK), BF),
            pltpu.VMEM((hd, BLK), BF), pltpu.VMEM((heads // 2, BLK, 4 * hd), BF),
            pltpu.VMEM((heads // 2, BLK, 4 * hd), BF), pltpu.VMEM((8, t), jnp.int32),
            pltpu.VMEM((t, d), BF), pltpu.SemaphoreType.DMA((1,)),
        ],
        compiler_params=params(),
        cost_estimate=cost(10 * heads * t * t * hd, 12 * MIB, heads * t * t),
        name="attention_backward",
    )(lens, half, q, k, v, sq, sk, pen, lse, dots, dmix, h1)


def first_kernel(cat, wqkv, wsel, out):
    wh = wqkv.shape[2]
    total = mm(cat[:, 3 * wh :], wsel[...])
    for i in range(3):
        total = total + mm_nt(cat[:, i * wh : (i + 1) * wh], wqkv[i])
    out[...] = total.astype(BF)


def first_grad(cat, wqkv, wsel):
    t, width = cat.shape
    d = wqkv.shape[1]
    return pl.pallas_call(
        first_kernel,
        grid=(t // BLK,),
        in_specs=[rows(width), whole(*wqkv.shape), whole(*wsel.shape)],
        out_specs=rows(d),
        out_shape=shape((t, d), BF),
        compiler_params=params(),
        cost_estimate=cost(2 * t * d * width, 6 * MIB, share=SHARES[0]),
        name="first_norm_grad",
    )(cat, wqkv, wsel)


def finish_kernel(
    x, part_a, part_b, gains, dmid, mid, fold_a, fold_b, grad_o, out_o, gain_o
):
    values = x[...].astype(F32)
    grad = part_a[...].astype(F32) + part_b[...].astype(F32)
    back, gain_grad = norm_back(values, norm_scale(values), gains[0:1, :], grad)
    grad_o[...] = dmid[...] + back
    out_o[...] = (mid[...] + (fold_a[...].astype(F32) + fold_b[...].astype(F32))).astype(BF)

    @pl.when(pl.program_id(0) == 0)
    def _():
        gain_o[...] = jnp.zeros_like(gain_o)

    gain_o[0:1, :] += gain_grad


def finish(x, part_a, part_b, gains, dmid, mid, fold_a, fold_b):
    t, d = x.shape
    return pl.pallas_call(
        finish_kernel,
        grid=(t // BLK,),
        in_specs=[rows(d), rows(d), rows(d), whole(*gains.shape)] + [rows(d)] * 4,
        out_specs=[rows(d), rows(d), whole(8, d)],
        out_shape=[shape((t, d), F32), shape((t, d), BF), shape((8, d), F32)],
        compiler_params=params(),
        cost_estimate=cost(24 * t * d, 20 * MIB, share=SHARES[2]),
        name="first_norm_backward",
    )(x, part_a, part_b, gains, dmid, mid, fold_a, fold_b)


def branch_kernel(act, down, out):
    out[...] = mm(act[...], down[...]).astype(BF)


def branch(act, down):
    t, hidden = act.shape
    d = down.shape[1]
    return pl.pallas_call(
        branch_kernel,
        grid=(t // BLK,),
        in_specs=[rows(hidden), whole(*down.shape)],
        out_specs=rows(d),
        out_shape=shape((t, d), BF),
        compiler_params=params(),
        cost_estimate=cost(2 * t * d * hidden, 8 * MIB, share=SHARES[1]),
        name="down_projection",
    )(act, down)


class Sum:
    def __init__(self, n_dp, n_tensor, orders):
        self.n_dp, self.n_tensor = n_dp, n_tensor
        self.stages = n_dp.bit_length() - 1
        rest = list(range(4, self.stages))
        self.orders = [[1 << b for b in list(orders[t % 2]) + rest] for t in range(n_tensor)]
        self.dp = lax.axis_index("dp")
        self.tensor = lax.axis_index("tensor")

    def place(self, stage):
        out = (self.dp // self.orders[0][stage]) % 2
        for t in range(1, self.n_tensor):
            out = jnp.where(self.tensor == t, (self.dp // self.orders[t][stage]) % 2, out)
        return out

    def swap(self, value, stage):
        pairs = [
            (i * self.n_tensor + t, (i ^ self.orders[t][stage]) * self.n_tensor + t)
            for i in range(self.n_dp)
            for t in range(self.n_tensor)
        ]
        return lax.ppermute(value, ("dp", "tensor"), pairs)

    def split(self, stage, *terms):
        size = terms[0].shape[0] // 2
        place = self.place(stage)

        def cut(which):
            pieces = [lax.dynamic_slice_in_dim(v, which * size, size, 0) for v in terms]
            return (pieces[0].astype(F32) + pieces[1].astype(F32)).astype(BF)

        return [cut(1 - place), cut(place)]

    def join(self, stage, mine, other):
        place = self.place(stage)
        low, high = jnp.where(place == 0, mine, other), jnp.where(place == 0, other, mine)
        return jnp.concatenate([low, high], axis=0)


class Chain:
    def __init__(self, sums, line):
        self.sums, self.line, self.stage = sums, line, 0

    def begin(self, send):
        self.got = self.sums.swap(send, 0)

    def hold(self, keep):
        self.keep = keep

    def reduce(self):
        sums, self.stage = self.sums, self.stage + 1
        if self.stage < sums.stages:
            split = functools.partial(sums.split, self.stage)
            send, self.keep = self.line.run(split, self.keep, self.got)
            self.got = sums.swap(send, self.stage)
        else:
            add = lambda a, b: [(a.astype(F32) + b.astype(F32)).astype(BF)]
            (self.piece,) = self.line.run(add, self.keep, self.got)
            self.spread()

    def spread(self):
        self.stage -= 1
        self.got = self.sums.swap(self.piece, self.stage)

    def gather(self):
        join = lambda *v: [self.sums.join(self.stage, *v)]
        (self.piece,) = self.line.run(join, self.piece, self.got)
        self.spread()

    def step(self):
        if not hasattr(self, "piece"):
            self.reduce()
        elif self.stage > 0:
            self.gather()
        else:
            return False
        return True

    def halves(self):
        return self.piece, self.got


class Line:
    def __init__(self):
        self.token = None

    def run(self, step, *values, after=()):
        if self.token is not None:
            first, *_ = lax.optimization_barrier((values[0], self.token, *after))
            values = (first, *values[1:])
        out = step(*values)
        self.token = out[0]
        return out


def swap_tensor(value, n_tensor):
    return lax.ppermute(value, "tensor", [(t, t ^ 1) for t in range(n_tensor)])


def join_kernel(side, mine, other, out):
    @pl.when(pl.program_id(0) == 0)
    def _():
        out[...] = mine[...].astype(F32)

    @pl.when(pl.program_id(0) == 1)
    def _():
        out[...] = other[...].astype(F32)


def join(side, mine, other):
    r, n = mine.shape
    tiles = 3
    tile = r // tiles
    return pl.pallas_call(
        join_kernel,
        grid_spec=pltpu.PrefetchScalarGridSpec(
            num_scalar_prefetch=1,
            grid=(2, tiles),
            in_specs=[
                pl.BlockSpec((tile, n), lambda s, j, side: (jnp.where(s == 0, j, tiles - 1), 0)),
                pl.BlockSpec((tile, n), lambda s, j, side: (jnp.where(s == 0, 0, j), 0)),
            ],
            out_specs=pl.BlockSpec(
                (tile, n), lambda s, j, side: (jnp.where(s == 0, side[0], 1 - side[0]) * tiles + j, 0)
            ),
        ),
        out_shape=shape((2 * r, n), F32),
        compiler_params=pltpu.CompilerParams(
            dimension_semantics=("arbitrary", "arbitrary"), vmem_limit_bytes=32 * MIB
        ),
        cost_estimate=cost(0, 12 * r * n, share=SHARES[3]),
        name="join_halves",
    )(side, mine, other)


def join_up_kernel(side, mine, other, up_o, out_o):
    def put(piece):
        up_o[...] = piece[:, : up_o.shape[1]].astype(F32)
        out_o[...] = piece[:, up_o.shape[1] :].astype(F32)

    pl.when(pl.program_id(0) == 0)(lambda: put(mine[...]))
    pl.when(pl.program_id(0) == 1)(lambda: put(other[...]))


def join_up(side, mine, other, hidden, wh):
    r, n = mine.shape
    place = lambda s, side: jnp.where(s == 0, side[0], 1 - side[0])
    return pl.pallas_call(
        join_up_kernel,
        grid_spec=pltpu.PrefetchScalarGridSpec(
            num_scalar_prefetch=1,
            grid=(2,),
            in_specs=[pl.BlockSpec((r, n), lambda s, side: (0, 0))] * 2,
            out_specs=[
                pl.BlockSpec((r, hidden), lambda s, side: (place(s, side), 0)),
                pl.BlockSpec((wh, r), lambda s, side: (0, place(s, side))),
            ],
        ),
        out_shape=[shape((2 * r, hidden), F32), shape((wh, 2 * r), F32)],
        compiler_params=params(32),
        cost_estimate=cost(0, 12 * r * n, share=SHARES[4]),
        name="join_up",
    )(side, mine, other)


def join_attention_kernel(wh, side, mine, other, qkv_o, sel_o):
    def put(piece):
        for i in range(3):
            qkv_o[i] = piece[:, i * wh : (i + 1) * wh].astype(F32)
        sel_o[...] = piece[:, 3 * wh :].astype(F32)

    pl.when(pl.program_id(0) == 0)(lambda: put(mine[...]))
    pl.when(pl.program_id(0) == 1)(lambda: put(other[...]))


def join_attention(side, mine, other, wh, hd):
    r, n = mine.shape
    place = lambda s, side: jnp.where(s == 0, side[0], 1 - side[0])
    return pl.pallas_call(
        functools.partial(join_attention_kernel, wh),
        grid_spec=pltpu.PrefetchScalarGridSpec(
            num_scalar_prefetch=1,
            grid=(2,),
            in_specs=[pl.BlockSpec((r, n), lambda s, side: (0, 0))] * 2,
            out_specs=[
                pl.BlockSpec((3, r, wh), lambda s, side: (0, place(s, side), 0)),
                pl.BlockSpec((r, 2 * hd), lambda s, side: (place(s, side), 0)),
            ],
        ),
        out_shape=[shape((3, 2 * r, wh), F32), shape((2 * r, 2 * hd), F32)],
        compiler_params=params(32),
        cost_estimate=cost(0, 12 * r * n, share=SHARES[5]),
        name="join_attention",
    )(side, mine, other)


def per_device(
    n_dp, n_tensor, inputs, seq_lengths, qkv_weight, out_weight, up_weight, down_weight,
    select_weight, norm_gains, grad_output,
):
    wh = qkv_weight.shape[2]
    hd = select_weight.shape[2]
    d = inputs.shape[1]
    hidden = up_weight.shape[1]
    line = Line()
    run = line.run
    sums = [Sum(n_dp, n_tensor, orders) for orders in (DOWN, UP, ATT)]
    down, up, att = (Chain(each, line) for each in sums)
    small = sums[0]
    down_kept, up_kept, att_kept = (
        each.place(0).reshape(1).astype(jnp.int32) for each in sums
    )
    select_t = jnp.swapaxes(select_weight, 1, 2)
    swap = functools.partial(swap_tensor, n_tensor=n_tensor)

    h1, q, k, v, sq, sk, pen, lse, mixed, part = run(
        forward, seq_lengths, inputs, norm_gains, qkv_weight, select_t, out_weight
    )
    mid, h2, act, du, dn2, down_send = run(
        lambda part, *v: feed(1 - down_kept, inputs, part, *v),
        part, swap(part), norm_gains, up_weight, down_weight, grad_output,
    )
    dn2_other = swap(dn2)
    down.begin(down_send)
    down.hold(*run(lambda act, *v: [down_half(down_kept, act, *v)], act, grad_output))
    dmid, dmix, dots, up_send, up_keep, gain_two = run(
        lambda dn2, *v: middle(1 - up_kept, mid, dn2, *v, hd),
        dn2, dn2_other, norm_gains, grad_output, out_weight, mixed, h2, du,
    )
    up.begin(up_send)
    up.hold(up_keep)
    steps = {"d": down.step, "u": up.step, "a": att.step}
    for letter in EARLY:
        steps[letter]()
    cat, att_send, att_keep = run(
        lambda dots, *v: backward(seq_lengths, 1 - att_kept, *v[:7], dots, *v[7:]),
        dots, q, k, v, sq, sk, pen, lse, dmix, h1,
    )
    att.begin(att_send)
    att.hold(att_keep)
    done = {}

    def first():
        value = (first_grad if FREE else over(first_grad))(cat, qkv_weight, select_t.reshape(2 * hd, d))
        done["dn1"] = value, swap(value)

    def fold():
        value = (branch if FREE else over(branch))(act, down_weight)
        done["fold"] = value, swap(value)

    def over(kernel):
        return lambda *v: run(lambda *w: [kernel(*w)], *v)[0]

    def last():
        done["inputs"], done["output"], gain_one = run(
            lambda dn1, *v: finish(inputs, dn1, *v),
            *done["dn1"], norm_gains, dmid, mid, *done["fold"],
        )
        done["gains"] = jnp.concatenate([gain_one[0:1], gain_two[0:1]], axis=0), 0

    def gain():
        value, stage = done["gains"]
        if stage == small.stages:
            return False
        (value,) = run(lambda *v: [v[0] + v[1]], value, small.swap(value, stage))
        done["gains"] = value, stage + 1
        return True

    def down_out():
        while down.step():
            pass
        (done["down"],) = run(lambda *v: [join(down_kept, *v)], *down.halves())

    def up_out():
        while up.step():
            pass
        done["up"] = run(lambda *v: join_up(up_kept, *v, hidden, wh), *up.halves())

    def att_out():
        while att.step():
            pass
        done["att"] = run(lambda *v: join_attention(att_kept, *v, wh, hd), *att.halves())

    steps.update(n=first, b=fold, f=last, g=gain, D=down_out, U=up_out, A=att_out)
    for letter in LATE:
        steps[letter]()
    while gain():
        pass
    grad_inputs, output, gains, grad_down = (done[k] for k in ("inputs", "output", "gains", "down"))
    gains = gains[0]
    grad_up, grad_out = done["up"]
    grad_qkv, select_part = done["att"]
    select_t_sum = select_part.T
    select_t_sum = select_t_sum + swap(select_t_sum)
    grad_select = jnp.swapaxes(select_t_sum.reshape(2, hd, d), 1, 2)
    return (output, grad_inputs, grad_qkv, grad_out, grad_up, grad_down, grad_select, gains)


def solution(mesh):
    placed = (
        P("dp", None),
        P("dp", None),
        P(None, None, "tensor"),
        P("tensor", None),
        P(None, "tensor"),
        P("tensor", None),
        P(),
        P(),
        P("dp", None),
    )
    return jax.shard_map(
        functools.partial(per_device, mesh.shape["dp"], mesh.shape["tensor"]),
        mesh=mesh,
        in_specs=placed,
        out_specs=(
            P("dp", None),
            P("dp", None),
            P(None, None, "tensor"),
            P("tensor", None),
            P(None, "tensor"),
            P("tensor", None),
            P(),
            P(),
        ),
        check_vma=False,
    )
```

```python
import functools

import jax
import jax.numpy as jnp
from jax import lax
from jax.experimental import pallas as pl
from jax.experimental.pallas import tpu as pltpu
from jax.sharding import PartitionSpec as P

BF = jnp.bfloat16
F32 = jnp.float32
EPS = 1e-6
BLK = 256
NOT_ATTENDED = 1e30
CURVE = 0.7978845608028654
CUBE = 0.044715
MIB = 1024 * 1024
COST = 1.0

DOWN = (0, 1, 2, 3), (1, 2, 0, 3)
UP = (2, 0, 1, 3), (1, 2, 0, 3)
ATT = (0, 1, 2, 3), (2, 0, 1, 3)
EARLY = "d"
LATE = "dbudnudaufuadaudaugadugaagDgAU"
FREE = False

SHARES = (3.0, 3.0, 3.0, 3.0, 3.0, 3.0)


def mm(a, b):
    return jnp.dot(a, b, preferred_element_type=F32)


def mm_nt(a, b):
    return lax.dot_general(a, b, (((1,), (1,)), ((), ())), preferred_element_type=F32)


def mm_tn(a, b):
    return lax.dot_general(a, b, (((0,), (0,)), ((), ())), preferred_element_type=F32)


def params(limit_mib=56):
    return pltpu.CompilerParams(
        dimension_semantics=("arbitrary",), vmem_limit_bytes=limit_mib * MIB
    )


def cost(flops, nbytes, trans=0, share=1.0):
    return pl.CostEstimate(
        flops=int(COST * share * flops), bytes_accessed=int(COST * share * nbytes),
        transcendentals=int(COST * share * trans),
    )


def shape(dims, dtype):
    return jax.ShapeDtypeStruct(tuple(dims), dtype)


def whole(*dims):
    return pl.BlockSpec(tuple(dims), lambda *_: (0,) * len(dims))


def rows(width, count=BLK):
    return pl.BlockSpec((count, width), lambda i, *_: (i, 0))


def anywhere():
    return pl.BlockSpec(memory_space=pl.ANY)


def fetch(start, wait, *copies):
    for condition, act in ((start, "start"), (wait, "wait")):
        if condition is None:
            continue

        @pl.when(condition)
        def _():
            for copy in copies:
                getattr(pltpu.make_async_copy(*copy), act)()


def smem():
    return pl.BlockSpec(memory_space=pltpu.SMEM)


def sequence_ids(lens, pos):
    seg = jnp.zeros(pos.shape, jnp.int32)
    first = jnp.zeros(pos.shape, jnp.bool_)
    end = jnp.int32(0)
    for s in range(lens.shape[1]):
        length = lens[0, s]
        first = first | ((pos == end) & (length > 0))
        end = end + length
        seg = seg + (pos >= end).astype(jnp.int32)
    seg = jnp.where(pos < end, seg, lens.shape[1] + 1 + pos)
    return seg, first


def split_dot(values, ones):
    high = values.astype(BF)
    low = (values - high.astype(F32)).astype(BF)
    return mm(high, ones) + mm(low, ones)


def norm_scale(values):
    return lax.rsqrt(jnp.mean(values * values, axis=-1, keepdims=True) + EPS)


def rows_of(i):
    return pl.ds(pl.multiple_of(i * BLK, BLK), BLK)


def triangle(later):
    first = lax.broadcasted_iota(jnp.int32, (BLK, BLK), 0)
    second = lax.broadcasted_iota(jnp.int32, (BLK, BLK), 1)
    return jnp.where(first > second if later else first < second, 1.0, 0.0).astype(BF)


def forward_kernel(
    heads, lens, x, gains, wqkv, wsel_t, wout,
    h1_o, q_o, k_o, v_o, sq_o, sk_o, pen_o, lse_o, mix_o, part_o,
    k_s, vt_s, sk_s, carry_s, qx_s, seg_s, top_s, sum_s, acc_s,
):
    step = pl.program_id(0)
    hd = wsel_t.shape[1]
    t = k_s.shape[0]
    two = 2 * hd
    pairs = heads // 2
    scale = hd**-0.5
    here = rows_of(step)

    @pl.when(step == 0)
    def _():
        carry_s[...] = jnp.zeros_like(carry_s)
        qx_s[...] = jnp.zeros_like(qx_s)
        seg, first = sequence_ids(lens, lax.broadcasted_iota(jnp.int32, (t, 1), 0))
        seg_s[:, 0:1] = seg
        seg_s[:, 1:2] = jnp.where(first, -1, seg)

    xf = x[...].astype(F32)
    h1 = (xf * norm_scale(xf) * gains[0:1, :]).astype(BF)
    h1_o[...] = h1
    q32, k32, v32 = (mm(h1, wqkv[i]) for i in range(3))
    sq32, sk32 = (mm_nt(h1, wsel_t[i]) for i in range(2))
    q = (q32.astype(BF) * scale).astype(BF)
    q_t = (q32.T.astype(BF) * scale).astype(BF)
    k = k32.astype(BF)
    sq = (sq32.astype(BF) * scale).astype(BF)
    sk = sk32.astype(BF)
    q_o[...] = q
    k_o[...] = k
    v_o[...] = v32.astype(BF)
    sq_o[...] = sq
    sk_o[...] = sk
    k_s[here, :] = k
    sk_s[here, :] = sk
    vt_s[:, here] = v32.T.astype(BF)
    for p in range(pairs):
        for side in range(2):
            h = 2 * p + side
            qx_s[p, side * hd : (side + 1) * hd, side * BLK : (side + 1) * BLK] = q_t[
                h * hd : (h + 1) * hd, :
            ]

    row = step * BLK + lax.broadcasted_iota(jnp.int32, (1, BLK), 1)
    seg_i, _ = sequence_ids(lens, row)
    before = triangle(False)
    top_s[...] = jnp.full_like(top_s, -NOT_ATTENDED)
    sum_s[...] = jnp.zeros_like(sum_s)
    acc_s[...] = jnp.zeros_like(acc_s)

    def tile(j, _):
        at = rows_of(j)
        raw = [mm(k_s[at, p * two : (p + 1) * two], qx_s[p]) for p in range(pairs)]
        col = j * BLK + lax.broadcasted_iota(jnp.int32, (BLK, 1), 0)
        sel = jnp.maximum(mm_nt(sk_s[at, :], sq), 0.0)
        picked = jnp.where((seg_s[at, 1:2] == seg_i) & (col < row), sel * sel, 0.0)
        pen = split_dot(picked, before) + carry_s[at, 0:1]
        carry_s[at, 0:1] = pen[:, BLK - 1 : BLK] + picked[:, BLK - 1 : BLK]
        bias = jnp.where((seg_s[at, 0:1] == seg_i) & (col <= row), pen, NOT_ATTENDED)
        pen_o[at, :] = bias
        bias = jnp.concatenate([bias, bias], axis=1)
        lows, fades = [], []
        for p in range(pairs):
            s = raw[p] - bias
            old = top_s[p : p + 1, :]
            top = jnp.maximum(old, jnp.max(s, axis=0, keepdims=True))
            fade = jnp.exp(old - top)
            prob = jnp.exp(s - top)
            top_s[p : p + 1, :] = top
            sum_s[p : p + 1, :] = sum_s[p : p + 1, :] * fade + jnp.sum(prob, axis=0, keepdims=True)
            lows.append(prob.astype(BF))
            fades.append(fade)
        for h in range(heads):
            p, cut = h // 2, slice((h % 2) * BLK, (h % 2 + 1) * BLK)
            mine = slice(h * hd, (h + 1) * hd)
            acc_s[mine, :] = acc_s[mine, :] * fades[p][:, cut] + mm(vt_s[mine, at], lows[p][:, cut])
        return 0

    lax.fori_loop(0, step + 1, tile, 0)
    for h in range(heads):
        p, cut = h // 2, slice((h % 2) * BLK, (h % 2 + 1) * BLK)
        total = sum_s[p : p + 1, cut]
        lse_o[h : h + 1, :] = top_s[p : p + 1, cut] + jnp.log(total)
        acc_s[h * hd : (h + 1) * hd, :] = acc_s[h * hd : (h + 1) * hd, :] / total
    mixed = acc_s[...].T.astype(BF)
    mix_o[...] = mixed
    part_o[...] = mm(mixed, wout[...]).astype(BF)


def forward(lens, x, gains, wqkv, wsel_t, wout):
    t, d = x.shape
    wh = wqkv.shape[2]
    hd = wsel_t.shape[1]
    heads = wh // hd
    n = t // BLK
    tall = pl.BlockSpec((t, BLK), lambda i: (0, i))
    return pl.pallas_call(
        functools.partial(forward_kernel, heads),
        grid=(n,),
        in_specs=[
            smem(), rows(d), whole(*gains.shape), whole(*wqkv.shape), whole(*wsel_t.shape),
            whole(*wout.shape),
        ],
        out_specs=[
            rows(d), rows(wh), rows(wh), rows(wh), rows(hd), rows(hd), tall,
            pl.BlockSpec((8, BLK), lambda i: (0, i)), rows(wh), rows(d),
        ],
        out_shape=[
            shape((t, d), BF), shape((t, wh), BF), shape((t, wh), BF), shape((t, wh), BF),
            shape((t, hd), BF), shape((t, hd), BF), shape((t, t), F32), shape((8, t), F32),
            shape((t, wh), BF), shape((t, d), BF),
        ],
        scratch_shapes=[
            pltpu.VMEM((t, wh), BF), pltpu.VMEM((wh, t), BF), pltpu.VMEM((t, hd), BF),
            pltpu.VMEM((t, 128), F32), pltpu.VMEM((heads // 2, 2 * hd, 2 * BLK), BF),
            pltpu.VMEM((t, 128), jnp.int32), pltpu.VMEM((8, 2 * BLK), F32),
            pltpu.VMEM((8, 2 * BLK), F32), pltpu.VMEM((wh, BLK), F32),
        ],
        compiler_params=params(),
        cost_estimate=cost(2 * t * d * (4 * wh + 2 * hd) + 4 * heads * t * t * hd, 16 * MIB, heads * t * t),
        name="attention_forward",
    )(lens, x, gains, wqkv, wsel_t, wout)


def feed_kernel(
    half, x, part_a, part_b, gains, up, down, g, mid_o, h2_o, act_o, du_o, dn_o, dsend_o,
    act_s,
):
    step = pl.program_id(0)
    here = rows_of(step)
    mid = x[...].astype(F32) + (part_a[...].astype(F32) + part_b[...].astype(F32))
    mid_o[...] = mid
    h2 = (mid * norm_scale(mid) * gains[1:2, :]).astype(BF)
    h2_o[...] = h2
    hidden = up.shape[1]
    chunk = hidden
    cuts = [slice(c, c + chunk) for c in range(0, hidden, chunk)]
    ups = [mm(h2, up[:, cut]) for cut in cuts]
    das = [mm_nt(g[here, :], down[cut, :]) for cut in cuts]
    dus = []
    for u, da, cut in zip(ups, das, cuts):
        u2 = u * u
        curve = jnp.tanh(u * (CURVE + (CURVE * CUBE) * u2))
        part = 0.5 * (1.0 + curve)
        act = (u * part).astype(BF)
        slope = part + (0.5 * u) * (1.0 - curve * curve) * (CURVE + (3.0 * CURVE * CUBE) * u2)
        du = (da * slope).astype(BF)
        act_o[:, cut] = act
        act_s[here, cut] = act
        du_o[:, cut] = du
        dus.append(du)
    dn = functools.reduce(jnp.add, [mm_nt(du, up[:, cut]) for du, cut in zip(dus, cuts)])
    dn_o[...] = dn.astype(BF)

    @pl.when(step == pl.num_programs(0) - 1)
    def _():
        size = dsend_o.shape[0]
        at = pl.ds(pl.multiple_of(half[0] * size, 128), size)
        dsend_o[...] = mm_tn(act_s[:, at], g[...]).astype(BF)


def feed(half, x, part_a, part_b, gains, up, down, g):
    t, d = x.shape
    hidden = up.shape[1]
    return pl.pallas_call(
        feed_kernel,
        grid=(t // BLK,),
        in_specs=[
            smem(), rows(d), rows(d), rows(d), whole(*gains.shape), whole(*up.shape),
            whole(*down.shape), whole(t, d),
        ],
        out_specs=[
            rows(d), rows(d), rows(hidden), rows(hidden), rows(d), whole(hidden // 2, d),
        ],
        out_shape=[
            shape((t, d), F32), shape((t, d), BF), shape((t, hidden), BF), shape((t, hidden), BF),
            shape((t, d), BF), shape((hidden // 2, d), BF),
        ],
        scratch_shapes=[pltpu.VMEM((t, hidden), BF)],
        compiler_params=params(),
        cost_estimate=cost(8 * t * d * hidden, 24 * MIB, t * hidden),
        name="feed_forward",
    )(half, x, part_a, part_b, gains, up, down, g)


def product_kernel(half, left, right, out):
    out[...] = mm_tn(left[...], right[...]).astype(BF)


def down_half(half, act, g):
    t, hidden = act.shape
    d = g.shape[1]
    tiles = 3
    tile = hidden // 2 // tiles
    return pl.pallas_call(
        product_kernel,
        grid_spec=pltpu.PrefetchScalarGridSpec(
            num_scalar_prefetch=1,
            grid=(tiles,),
            in_specs=[
                pl.BlockSpec((t, tile), lambda j, half: (0, half[0] * tiles + j)),
                whole(t, d),
            ],
            out_specs=pl.BlockSpec((tile, d), lambda j, half: (j, 0)),
        ),
        out_shape=shape((hidden // 2, d), BF),
        compiler_params=params(),
        cost_estimate=cost(t * d * hidden, 6 * MIB),
        name="grad_down",
    )(half, act, g)


def norm_back(values, scale, gain, grad):
    unit = values * scale
    grad_unit = grad * gain
    mean = jnp.mean(grad_unit * unit, axis=-1, keepdims=True)
    return scale * (grad_unit - unit * mean), jnp.sum(grad * unit, axis=0, keepdims=True)


def middle_kernel(
    hd, half, mid, part_a, part_b, gains, g, wout, mixed_row, mixed_in, h2_in, du_in, dmid_o,
    dmix_o, dots_o, send_o, keep_o, gain_o, gm_s, mixed, h2, du, sems,
):
    step = pl.program_id(0)
    here = rows_of(step)
    final = step == pl.num_programs(0) - 1
    late = [
        (source, target, sems.at[n])
        for n, (source, target) in enumerate(((h2_in, h2), (du_in, du), (mixed_in, mixed)))
    ]
    fetch(step == 0, None, *late)
    values = mid[...]
    grad = part_a[...].astype(F32) + part_b[...].astype(F32)
    back, gain_grad = norm_back(values, norm_scale(values), gains[1:2, :], grad)
    dmid = g[...].astype(F32) + back
    dmid_o[...] = dmid
    gm = dmid.astype(BF)
    gm_s[here, :] = gm
    dmix = mm_nt(gm, wout[...]).astype(BF)
    dmix_o[...] = dmix
    both = (dmix.astype(F32) * mixed_row[...].astype(F32)).T
    for h in range(both.shape[0] // hd):
        dots_o[h : h + 1, :] = jnp.sum(both[h * hd : (h + 1) * hd, :], axis=0, keepdims=True)

    @pl.when(step == 0)
    def _():
        gain_o[...] = jnp.zeros_like(gain_o)

    gain_o[0:1, :] += gain_grad
    fetch(None, final, *late)

    @pl.when(final)
    def _():
        hidden = du.shape[1]
        size = send_o.shape[0]
        for which, into in ((half[0], send_o), (1 - half[0], keep_o)):
            at = pl.ds(pl.multiple_of(which * size, 128), size)
            into[:, :hidden] = mm_tn(h2[:, at], du[...]).astype(BF)
            into[:, hidden:] = mm_tn(mixed[...], gm_s[:, at]).astype(BF)


def middle(half, mid, part_a, part_b, gains, g, wout, mixed, h2, du, hd):
    t, d = mid.shape
    wh = wout.shape[0]
    hidden = du.shape[1]
    return pl.pallas_call(
        functools.partial(middle_kernel, hd),
        grid=(t // BLK,),
        in_specs=[
            smem(), rows(d), rows(d), rows(d), whole(*gains.shape), rows(d), whole(*wout.shape),
            rows(wh), anywhere(), anywhere(), anywhere(),
        ],
        out_specs=[
            rows(d), rows(wh), pl.BlockSpec((8, BLK), lambda i: (0, i)),
            whole(d // 2, hidden + d // 2), whole(d // 2, hidden + d // 2), whole(8, d),
        ],
        out_shape=[
            shape((t, d), F32), shape((t, wh), BF), shape((8, t), F32),
            shape((d // 2, hidden + d // 2), BF), shape((d // 2, hidden + d // 2), BF),
            shape((8, d), F32),
        ],
        scratch_shapes=[
            pltpu.VMEM((t, d), BF), pltpu.VMEM((t, wh), BF), pltpu.VMEM((t, d), BF),
            pltpu.VMEM((t, hidden), BF), pltpu.SemaphoreType.DMA((3,)),
        ],
        compiler_params=params(),
        cost_estimate=cost(2 * t * d * wh + t * d * hidden, 20 * MIB),
        name="second_norm_backward",
    )(half, mid, part_a, part_b, gains, g, wout, mixed, mixed, h2, du)


def split_three(values):
    one = values.astype(BF).astype(F32)
    rest = values - one
    two = rest.astype(BF).astype(F32)
    return one, two, (rest - two).astype(BF).astype(F32)


def backward_kernel(
    n_blocks, heads, lens, half, q, k, v, sq, sk, pen, lse, dots, dmix, h1_in, cat_o, send_o, keep_o,
    qx_s, qm_s, dx_s, dm_s, dq_s, dsq_s, dk_s, dv_s, dsk_s, kt_s, skt_s, kx_s, vx_s, seg_s, h1, sems,
):
    j = pl.program_id(0)
    late = (h1_in, h1, sems.at[0])
    fetch(j == 0, None, late)
    wh = k.shape[1]
    hd = sk.shape[1]
    t = q.shape[0]
    two = 2 * hd
    pairs = heads // 2
    scale = hd**-0.5
    lane = lax.broadcasted_iota(jnp.int32, (1, two), 1)
    side_of = [lane // hd == side for side in range(2)]
    ones = jnp.broadcast_to(jnp.where(lane < 3, 1.0, 0.0).astype(BF), (BLK, two))

    @pl.when(j == 0)
    def _():
        dq_s[...] = jnp.zeros_like(dq_s)
        dsq_s[...] = jnp.zeros_like(dsq_s)
        seg, _ = sequence_ids(lens, lax.broadcasted_iota(jnp.int32, (1, t), 1))
        seg_s[0:1, :] = seg

        tall = lax.broadcasted_iota(jnp.int32, (two, 1), 0)

        def prepare(i, _):
            at = rows_of(i)
            for which, (source, plain, wide) in enumerate(((q, qm_s, qx_s), (dmix, dm_s, dx_s))):
                source_t = source[at, :].astype(F32).T
                for h in range(heads):
                    side = h % 2
                    pair = slice((h // 2) * two, (h // 2 + 1) * two)
                    cut = slice(side * BLK, (side + 1) * BLK)
                    value = jnp.where(side_of[side], source[at, pair], jnp.zeros((), BF))
                    plain[h // 2, i, cut, :] = value
                    value = jnp.where(tall // hd == side, source_t[pair, :], 0.0)
                    wide[h // 2, i, 0:two, cut] = value.astype(BF)
                    one, mid, low = split_three(-(lse, dots)[which][h : h + 1, at])
                    value = jnp.where(tall == 0, one, jnp.where(tall == 1, mid, jnp.where(tall == 2, low, 0.0)))
                    wide[h // 2, i, two : 2 * two, cut] = value.astype(BF)
            return 0

        lax.fori_loop(0, n_blocks, prepare, 0)

    here = rows_of(j)
    dk_s[...] = jnp.zeros_like(dk_s)
    dv_s[...] = jnp.zeros_like(dv_s)
    dsk_s[...] = jnp.zeros_like(dsk_s)
    kt_s[...] = k[...].astype(F32).T.astype(BF)
    skt_s[...] = sk[...].astype(F32).T.astype(BF)
    for p in range(pairs):
        pair = slice(p * two, (p + 1) * two)
        kx_s[p, :, 0:two] = k[:, pair]
        vx_s[p, :, 0:two] = v[:, pair]
        kx_s[p, :, two:] = ones
        vx_s[p, :, two:] = ones
    after = triangle(True)
    col = j * BLK + lax.broadcasted_iota(jnp.int32, (BLK, 1), 0)
    seg_j, first_j = sequence_ids(lens, col)
    seg_j = jnp.where(first_j, -1, seg_j)

    def tile(back, carry):
        i = n_blocks - 1 - back
        at = rows_of(i)
        bias = pen[:, at]
        bias = jnp.concatenate([bias, bias], axis=1)
        scores = [mm(kx_s[p], qx_s[p, i]) - bias for p in range(pairs)]
        dprobs = [mm(vx_s[p], dx_s[p, i]) for p in range(pairs)]
        sel = jnp.maximum(mm_nt(sk[...], sq[at, :]), 0.0)
        dpen = None
        probs, lows = [], []
        for p in range(pairs):
            prob = jnp.exp(scores[p])
            dscore = prob * dprobs[p]
            both = dscore[:, :BLK] + dscore[:, BLK:]
            dpen = both if dpen is None else dpen + both
            probs.append(prob.astype(BF))
            lows.append(dscore.astype(BF))
        dpicked = split_dot(dpen, after) + carry
        for p in range(pairs):
            pair = slice(p * two, (p + 1) * two)
            for side in range(2):
                h = 2 * p + side
                dq_s[p, side * hd : (side + 1) * hd, at] += mm(
                    kt_s[h * hd : (h + 1) * hd, :], lows[p][:, side * BLK : (side + 1) * BLK]
                )
            dv_s[:, pair] += mm(probs[p], dm_s[p, i])
            dk_s[:, pair] += mm(lows[p], qm_s[p, i])
        row = i * BLK + lax.broadcasted_iota(jnp.int32, (1, BLK), 1)
        chosen = (seg_j == seg_s[0:1, at]) & (col < row)
        dsel = jnp.where(chosen, -2.0 * dpicked * sel, 0.0).astype(BF)
        dsk_s[...] += mm(dsel, sq[at, :])
        dsq_s[:, at] += mm(skt_s[...], dsel)
        return dpicked[:, 0:1] + dpen[:, 0:1]

    lax.fori_loop(0, n_blocks - j, tile, jnp.zeros((BLK, 1), F32))
    cat_o[here, wh : 2 * wh] = dk_s[...].astype(BF)
    cat_o[here, 2 * wh : 3 * wh] = dv_s[...].astype(BF)
    cat_o[here, 3 * wh + hd : 3 * wh + 2 * hd] = dsk_s[...].astype(BF)

    fetch(None, j == n_blocks - 1, late)

    @pl.when(j == n_blocks - 1)
    def _():
        for p in range(pairs):
            cat_o[:, p * two : (p + 1) * two] = (dq_s[p] * scale).T.astype(BF)
        cat_o[:, 3 * wh : 3 * wh + hd] = (dsq_s[...] * scale).T.astype(BF)
        size = send_o.shape[0]
        for which, into in ((half[0], send_o), (1 - half[0], keep_o)):
            at = pl.ds(pl.multiple_of(which * size, 128), size)
            into[...] = mm_tn(h1[:, at], cat_o[...]).astype(BF)


def backward(lens, half, q, k, v, sq, sk, pen, lse, dots, dmix, h1):
    d = h1.shape[1]
    t, wh = q.shape
    hd = sq.shape[1]
    heads = wh // hd
    n = t // BLK
    width = 3 * wh + 2 * hd
    per_head = pltpu.VMEM((heads // 2, n, 2 * BLK, 2 * hd), BF)
    per_head_t = pltpu.VMEM((heads // 2, n, 4 * hd, 2 * BLK), BF)
    return pl.pallas_call(
        functools.partial(backward_kernel, n, heads),
        grid=(n,),
        in_specs=[
            smem(), smem(), whole(t, wh), rows(wh), rows(wh), whole(t, hd), rows(hd), rows(t),
            whole(8, t), whole(8, t), whole(t, wh), anywhere(),
        ],
        out_specs=[whole(t, width), whole(d // 2, width), whole(d // 2, width)],
        out_shape=[
            shape((t, width), BF), shape((d // 2, width), BF), shape((d // 2, width), BF),
        ],
        scratch_shapes=[
            per_head_t, per_head, per_head_t, per_head, pltpu.VMEM((heads // 2, 2 * hd, t), F32),
            pltpu.VMEM((hd, t), F32), pltpu.VMEM((BLK, wh), F32),
            pltpu.VMEM((BLK, wh), F32), pltpu.VMEM((BLK, hd), F32), pltpu.VMEM((wh, BLK), BF),
            pltpu.VMEM((hd, BLK), BF), pltpu.VMEM((heads // 2, BLK, 4 * hd), BF),
            pltpu.VMEM((heads // 2, BLK, 4 * hd), BF), pltpu.VMEM((8, t), jnp.int32),
            pltpu.VMEM((t, d), BF), pltpu.SemaphoreType.DMA((1,)),
        ],
        compiler_params=params(),
        cost_estimate=cost(10 * heads * t * t * hd, 12 * MIB, heads * t * t),
        name="attention_backward",
    )(lens, half, q, k, v, sq, sk, pen, lse, dots, dmix, h1)


def first_kernel(cat, wqkv, wsel, out):
    wh = wqkv.shape[2]
    total = mm(cat[:, 3 * wh :], wsel[...])
    for i in range(3):
        total = total + mm_nt(cat[:, i * wh : (i + 1) * wh], wqkv[i])
    out[...] = total.astype(BF)


def first_grad(cat, wqkv, wsel):
    t, width = cat.shape
    d = wqkv.shape[1]
    return pl.pallas_call(
        first_kernel,
        grid=(t // BLK,),
        in_specs=[rows(width), whole(*wqkv.shape), whole(*wsel.shape)],
        out_specs=rows(d),
        out_shape=shape((t, d), BF),
        compiler_params=params(),
        cost_estimate=cost(2 * t * d * width, 6 * MIB, share=SHARES[0]),
        name="first_norm_grad",
    )(cat, wqkv, wsel)


def finish_kernel(
    x, part_a, part_b, gains, dmid, mid, fold_a, fold_b, grad_o, out_o, gain_o
):
    values = x[...].astype(F32)
    grad = part_a[...].astype(F32) + part_b[...].astype(F32)
    back, gain_grad = norm_back(values, norm_scale(values), gains[0:1, :], grad)
    grad_o[...] = dmid[...] + back
    out_o[...] = (mid[...] + (fold_a[...].astype(F32) + fold_b[...].astype(F32))).astype(BF)

    @pl.when(pl.program_id(0) == 0)
    def _():
        gain_o[...] = jnp.zeros_like(gain_o)

    gain_o[0:1, :] += gain_grad


def finish(x, part_a, part_b, gains, dmid, mid, fold_a, fold_b):
    t, d = x.shape
    return pl.pallas_call(
        finish_kernel,
        grid=(t // BLK,),
        in_specs=[rows(d), rows(d), rows(d), whole(*gains.shape)] + [rows(d)] * 4,
        out_specs=[rows(d), rows(d), whole(8, d)],
        out_shape=[shape((t, d), F32), shape((t, d), BF), shape((8, d), F32)],
        compiler_params=params(),
        cost_estimate=cost(24 * t * d, 20 * MIB, share=SHARES[2]),
        name="first_norm_backward",
    )(x, part_a, part_b, gains, dmid, mid, fold_a, fold_b)


def branch_kernel(act, down, out):
    out[...] = mm(act[...], down[...]).astype(BF)


def branch(act, down):
    t, hidden = act.shape
    d = down.shape[1]
    return pl.pallas_call(
        branch_kernel,
        grid=(t // BLK,),
        in_specs=[rows(hidden), whole(*down.shape)],
        out_specs=rows(d),
        out_shape=shape((t, d), BF),
        compiler_params=params(),
        cost_estimate=cost(2 * t * d * hidden, 8 * MIB, share=SHARES[1]),
        name="down_projection",
    )(act, down)


class Sum:
    def __init__(self, n_dp, n_tensor, orders):
        self.n_dp, self.n_tensor = n_dp, n_tensor
        self.stages = n_dp.bit_length() - 1
        rest = list(range(4, self.stages))
        self.orders = [[1 << b for b in list(orders[t % 2]) + rest] for t in range(n_tensor)]
        self.dp = lax.axis_index("dp")
        self.tensor = lax.axis_index("tensor")

    def place(self, stage):
        out = (self.dp // self.orders[0][stage]) % 2
        for t in range(1, self.n_tensor):
            out = jnp.where(self.tensor == t, (self.dp // self.orders[t][stage]) % 2, out)
        return out

    def swap(self, value, stage):
        pairs = [
            (i * self.n_tensor + t, (i ^ self.orders[t][stage]) * self.n_tensor + t)
            for i in range(self.n_dp)
            for t in range(self.n_tensor)
        ]
        return lax.ppermute(value, ("dp", "tensor"), pairs)

    def split(self, stage, *terms):
        size = terms[0].shape[0] // 2
        place = self.place(stage)

        def cut(which):
            pieces = [lax.dynamic_slice_in_dim(v, which * size, size, 0) for v in terms]
            return (pieces[0].astype(F32) + pieces[1].astype(F32)).astype(BF)

        return [cut(1 - place), cut(place)]

    def join(self, stage, mine, other):
        place = self.place(stage)
        low, high = jnp.where(place == 0, mine, other), jnp.where(place == 0, other, mine)
        return jnp.concatenate([low, high], axis=0)


class Chain:
    def __init__(self, sums, line):
        self.sums, self.line, self.stage = sums, line, 0

    def begin(self, send):
        self.got = self.sums.swap(send, 0)

    def hold(self, keep):
        self.keep = keep

    def reduce(self):
        sums, self.stage = self.sums, self.stage + 1
        if self.stage < sums.stages:
            split = functools.partial(sums.split, self.stage)
            send, self.keep = self.line.run(split, self.keep, self.got)
            self.got = sums.swap(send, self.stage)
        else:
            add = lambda a, b: [(a.astype(F32) + b.astype(F32)).astype(BF)]
            (self.piece,) = self.line.run(add, self.keep, self.got)
            self.spread()

    def spread(self):
        self.stage -= 1
        self.got = self.sums.swap(self.piece, self.stage)

    def gather(self):
        join = lambda *v: [self.sums.join(self.stage, *v)]
        (self.piece,) = self.line.run(join, self.piece, self.got)
        self.spread()

    def step(self):
        if not hasattr(self, "piece"):
            self.reduce()
        elif self.stage > 0:
            self.gather()
        else:
            return False
        return True

    def halves(self):
        return self.piece, self.got


class Line:
    def __init__(self):
        self.token = None

    def run(self, step, *values, after=()):
        if self.token is not None:
            first, *_ = lax.optimization_barrier((values[0], self.token, *after))
            values = (first, *values[1:])
        out = step(*values)
        self.token = out[0]
        return out


def swap_tensor(value, n_tensor):
    return lax.ppermute(value, "tensor", [(t, t ^ 1) for t in range(n_tensor)])


def join_kernel(side, mine, other, out):
    @pl.when(pl.program_id(0) == 0)
    def _():
        out[...] = mine[...].astype(F32)

    @pl.when(pl.program_id(0) == 1)
    def _():
        out[...] = other[...].astype(F32)


def join(side, mine, other):
    r, n = mine.shape
    tiles = 3
    tile = r // tiles
    return pl.pallas_call(
        join_kernel,
        grid_spec=pltpu.PrefetchScalarGridSpec(
            num_scalar_prefetch=1,
            grid=(2, tiles),
            in_specs=[
                pl.BlockSpec((tile, n), lambda s, j, side: (jnp.where(s == 0, j, tiles - 1), 0)),
                pl.BlockSpec((tile, n), lambda s, j, side: (jnp.where(s == 0, 0, j), 0)),
            ],
            out_specs=pl.BlockSpec(
                (tile, n), lambda s, j, side: (jnp.where(s == 0, side[0], 1 - side[0]) * tiles + j, 0)
            ),
        ),
        out_shape=shape((2 * r, n), F32),
        compiler_params=pltpu.CompilerParams(
            dimension_semantics=("arbitrary", "arbitrary"), vmem_limit_bytes=32 * MIB
        ),
        cost_estimate=cost(0, 12 * r * n, share=SHARES[3]),
        name="join_halves",
    )(side, mine, other)


def join_up_kernel(side, mine, other, up_o, out_o):
    def put(piece):
        up_o[...] = piece[:, : up_o.shape[1]].astype(F32)
        out_o[...] = piece[:, up_o.shape[1] :].astype(F32)

    pl.when(pl.program_id(0) == 0)(lambda: put(mine[...]))
    pl.when(pl.program_id(0) == 1)(lambda: put(other[...]))


def join_up(side, mine, other, hidden, wh):
    r, n = mine.shape
    place = lambda s, side: jnp.where(s == 0, side[0], 1 - side[0])
    return pl.pallas_call(
        join_up_kernel,
        grid_spec=pltpu.PrefetchScalarGridSpec(
            num_scalar_prefetch=1,
            grid=(2,),
            in_specs=[pl.BlockSpec((r, n), lambda s, side: (0, 0))] * 2,
            out_specs=[
                pl.BlockSpec((r, hidden), lambda s, side: (place(s, side), 0)),
                pl.BlockSpec((wh, r), lambda s, side: (0, place(s, side))),
            ],
        ),
        out_shape=[shape((2 * r, hidden), F32), shape((wh, 2 * r), F32)],
        compiler_params=params(32),
        cost_estimate=cost(0, 12 * r * n, share=SHARES[4]),
        name="join_up",
    )(side, mine, other)


def join_attention_kernel(wh, side, mine, other, qkv_o, sel_o):
    def put(piece):
        for i in range(3):
            qkv_o[i] = piece[:, i * wh : (i + 1) * wh].astype(F32)
        sel_o[...] = piece[:, 3 * wh :].astype(F32).T

    pl.when(pl.program_id(0) == 0)(lambda: put(mine[...]))
    pl.when(pl.program_id(0) == 1)(lambda: put(other[...]))


def join_attention(side, mine, other, wh, hd):
    r, n = mine.shape
    place = lambda s, side: jnp.where(s == 0, side[0], 1 - side[0])
    return pl.pallas_call(
        functools.partial(join_attention_kernel, wh),
        grid_spec=pltpu.PrefetchScalarGridSpec(
            num_scalar_prefetch=1,
            grid=(2,),
            in_specs=[pl.BlockSpec((r, n), lambda s, side: (0, 0))] * 2,
            out_specs=[
                pl.BlockSpec((3, r, wh), lambda s, side: (0, place(s, side), 0)),
                pl.BlockSpec((2 * hd, r), lambda s, side: (0, place(s, side))),
            ],
        ),
        out_shape=[shape((3, 2 * r, wh), F32), shape((2 * hd, 2 * r), F32)],
        compiler_params=params(32),
        cost_estimate=cost(0, 12 * r * n, share=SHARES[5]),
        name="join_attention",
    )(side, mine, other)


def per_device(
    n_dp, n_tensor, inputs, seq_lengths, qkv_weight, out_weight, up_weight, down_weight,
    select_weight, norm_gains, grad_output,
):
    wh = qkv_weight.shape[2]
    hd = select_weight.shape[2]
    d = inputs.shape[1]
    hidden = up_weight.shape[1]
    line = Line()
    run = line.run
    sums = [Sum(n_dp, n_tensor, orders) for orders in (DOWN, UP, ATT)]
    down, up, att = (Chain(each, line) for each in sums)
    small = sums[0]
    down_kept, up_kept, att_kept = (
        each.place(0).reshape(1).astype(jnp.int32) for each in sums
    )
    select_t = jnp.swapaxes(select_weight, 1, 2)
    swap = functools.partial(swap_tensor, n_tensor=n_tensor)

    h1, q, k, v, sq, sk, pen, lse, mixed, part = run(
        forward, seq_lengths, inputs, norm_gains, qkv_weight, select_t, out_weight
    )
    mid, h2, act, du, dn2, down_send = run(
        lambda part, *v: feed(1 - down_kept, inputs, part, *v),
        part, swap(part), norm_gains, up_weight, down_weight, grad_output,
    )
    dn2_other = swap(dn2)
    down.begin(down_send)
    down.hold(*run(lambda act, *v: [down_half(down_kept, act, *v)], act, grad_output))
    dmid, dmix, dots, up_send, up_keep, gain_two = run(
        lambda dn2, *v: middle(1 - up_kept, mid, dn2, *v, hd),
        dn2, dn2_other, norm_gains, grad_output, out_weight, mixed, h2, du,
    )
    up.begin(up_send)
    up.hold(up_keep)
    steps = {"d": down.step, "u": up.step, "a": att.step}
    for letter in EARLY:
        steps[letter]()
    cat, att_send, att_keep = run(
        lambda dots, *v: backward(seq_lengths, 1 - att_kept, *v[:7], dots, *v[7:]),
        dots, q, k, v, sq, sk, pen, lse, dmix, h1,
    )
    att.begin(att_send)
    att.hold(att_keep)
    done = {}

    def first():
        value = (first_grad if FREE else over(first_grad))(cat, qkv_weight, select_t.reshape(2 * hd, d))
        done["dn1"] = value, swap(value)

    def fold():
        value = (branch if FREE else over(branch))(act, down_weight)
        done["fold"] = value, swap(value)

    def over(kernel):
        return lambda *v: run(lambda *w: [kernel(*w)], *v)[0]

    def last():
        done["inputs"], done["output"], gain_one = run(
            lambda dn1, *v: finish(inputs, dn1, *v),
            *done["dn1"], norm_gains, dmid, mid, *done["fold"],
        )
        done["gains"] = jnp.concatenate([gain_one[0:1], gain_two[0:1]], axis=0), 0

    def gain():
        value, stage = done["gains"]
        if stage == small.stages:
            return False
        (value,) = run(lambda *v: [v[0] + v[1]], value, small.swap(value, stage))
        done["gains"] = value, stage + 1
        return True

    def down_out():
        while down.step():
            pass
        (done["down"],) = run(lambda *v: [join(down_kept, *v)], *down.halves())

    def up_out():
        while up.step():
            pass
        done["up"] = run(lambda *v: join_up(up_kept, *v, hidden, wh), *up.halves())

    def att_out():
        while att.step():
            pass
        done["att"] = run(lambda *v: join_attention(att_kept, *v, wh, hd), *att.halves())

    steps.update(n=first, b=fold, f=last, g=gain, D=down_out, U=up_out, A=att_out)
    for letter in LATE:
        steps[letter]()
    while gain():
        pass
    grad_inputs, output, gains, grad_down = (done[k] for k in ("inputs", "output", "gains", "down"))
    gains = gains[0]
    grad_up, grad_out = done["up"]
    grad_qkv, select_part = done["att"]
    select_t_sum = select_part + swap(select_part)
    grad_select = jnp.swapaxes(select_t_sum.reshape(2, hd, d), 1, 2)
    return (output, grad_inputs, grad_qkv, grad_out, grad_up, grad_down, grad_select, gains)


def solution(mesh):
    placed = (
        P("dp", None),
        P("dp", None),
        P(None, None, "tensor"),
        P("tensor", None),
        P(None, "tensor"),
        P("tensor", None),
        P(),
        P(),
        P("dp", None),
    )
    return jax.shard_map(
        functools.partial(per_device, mesh.shape["dp"], mesh.shape["tensor"]),
        mesh=mesh,
        in_specs=placed,
        out_specs=(
            P("dp", None),
            P("dp", None),
            P(None, None, "tensor"),
            P("tensor", None),
            P(None, "tensor"),
            P("tensor", None),
            P(),
            P(),
        ),
        check_vma=False,
    )
```
